32 devices in a mesh: angle: 4 (over y, x), row: 8 (over z, core).
Axes of the slice: x: 2, y: 2, z: 4, core: 2. Of those that a mesh axis runs over, the one named last changes fastest.
Arguments:
- intensity: float32 [512, 8, 4096], P('angle', 'row'), may hold values from 0.036 to 1
- flat_field: float32 [8, 4096], P('row'), may hold values from 1 to 2
- dark_field: float32 [8, 4096], P('row'), may hold values from 0 to 0.02
- correlation: int32 [1], replicated, may hold values from 512 to 1536
- blend_width: int32 [1], replicated, may hold values from 64 to 511
- padding: int32 [1], replicated, may hold values from 1024 to 4096
- cutoff: int32 [1], replicated, may hold values from 1 to 8
Outputs:
- sinogram: float32 [256, 8, 8192], P('angle', 'row')
The draws below stay inside these ranges and needn't reach their ends.
All inputs are finite; a program needn't handle non-finite values.
Results may differ from the reference program's by a relative error of at most 0.00023.
Values sent between devices are 32-bit elements; how exact they have to be, the bound alone decides.
No kernel may reach another device: no remote copies, remote signals or barrier semaphores. Data moves between devices by JAX's collectives and lax.ppermute only.
A program may use at most 128 MiB of HBM per device.

```python
import math
import jax
import jax.numpy as jnp
from jax import lax

DET = 4096
HB = 64
KMAX = 8
HALF = 256
ANGLES = 512
ROWS = 8
FCUT = 512
OVL_LO = 512
OVL_HI = 1536
BLEND_LO = 64
BLEND_HI = 511
PAD_LO = 1024
PAD_HI = 4096
N_ANGLE = 4


def draw_intensity(key, part):
    noise_key, amp_key, phase_key = jax.random.split(key, 3)
    full_shape = (ANGLES, ROWS, DET)
    noise_factor = jax.random.uniform(noise_key, full_shape, jnp.float32, 0.4, 1.0)
    amplitude = jax.random.uniform(amp_key, (8, ROWS, DET), jnp.float32, 0.0, 0.15)
    phase_shift = jax.random.uniform(phase_key, (8, ROWS, DET), jnp.float32, -math.pi, math.pi)
    angle_index = jnp.arange(ANGLES, dtype=jnp.int32)
    exponent = jnp.zeros(full_shape, jnp.float32)
    for harmonic in range(1, 9):
        turn_angle = (harmonic * angle_index % HALF).astype(jnp.float32) * (2.0 * math.pi / HALF)
        exponent = exponent + amplitude[harmonic - 1] * (1.0 + jnp.cos(turn_angle[:, None, None] + phase_shift[harmonic - 1]))
    return noise_factor * jnp.exp(-exponent)


def levels(own_key, dims, shards, least, largest):
    loudness, own = 1.0, jax.random.fold_in(own_key, 6)
    for dim, parts in shards:
        steps = jnp.exp(jax.random.uniform(jax.random.fold_in(own, dim), (parts,), jnp.float32, least / len(shards), largest / len(shards)))
        loudness = loudness * jnp.repeat(steps, dims[dim] // parts).reshape([-1 if axis == dim else 1 for axis in range(len(dims))])
    return loudness


def setup_inputs(seed: int = 0) -> dict:
    arg_keys = jax.random.split(jax.random.key(seed), 8)
    return {
        "intensity": draw_intensity(jax.random.fold_in(arg_keys[7], 71), 0),
        "flat_field": jnp.clip(1.0 + 1.0 * jax.random.uniform(arg_keys[1], (ROWS, DET), jnp.float32) ** levels(arg_keys[1], (ROWS, DET), ((0, 8),), -0.2, 0.2), 1.0, 2.0),
        "dark_field": jnp.clip(0.02 * jax.random.uniform(arg_keys[2], (ROWS, DET), jnp.float32) ** levels(arg_keys[2], (ROWS, DET), ((0, 8),), -0.2, 0.2), 0.0, 0.02),
        "correlation": jax.random.randint(arg_keys[3], (1,), OVL_LO, OVL_HI + 1).astype(jnp.int32),
        "blend_width": jax.random.randint(arg_keys[4], (1,), BLEND_LO, BLEND_HI + 1).astype(jnp.int32),
        "padding": jax.random.randint(arg_keys[5], (1,), PAD_LO, PAD_HI + 1).astype(jnp.int32),
        "cutoff": jax.random.randint(arg_keys[6], (1,), 1, KMAX + 1).astype(jnp.int32),
    }


def stitch(main_view, back_view, correlation, blend_size):
    pixels = main_view.shape[-1]
    leading = main_view.shape[:-1]
    last_axis = main_view.ndim - 1
    empty = jnp.zeros(leading + (pixels,), main_view.dtype)
    edge_hold = jnp.broadcast_to(main_view[..., -1:], leading + (pixels,))
    extended_main = jnp.concatenate([empty, main_view, edge_hold], axis=-1)
    right_side = lax.dynamic_slice_in_dim(extended_main, correlation, 2 * pixels, last_axis)
    left_side = jnp.concatenate([jnp.flip(back_view, -1), empty], axis=-1)
    position = jnp.arange(2 * pixels).astype(main_view.dtype)
    center = pixels - correlation.astype(main_view.dtype) / 2.0
    weight_right = jnp.clip((position + 0.5 - center) / blend_size.astype(main_view.dtype) + 0.5, 0.0, 1.0)
    return left_side * (1.0 - weight_right) + right_side * weight_right


def extend(stitched, padding, length):
    width_now = stitched.shape[-1]
    leading = stitched.shape[:-1]
    base_row = jnp.concatenate([stitched, jnp.zeros(leading + (length - width_now,), stitched.dtype)], axis=-1)
    index_list = jnp.arange(length, dtype=jnp.int32)
    right_mask = (index_list >= width_now) & (index_list < width_now + padding)
    left_mask = index_list >= length - padding
    return base_row + jnp.where(right_mask, stitched[..., -1:], 0.0) + jnp.where(left_mask, stitched[..., :1], 0.0)


def reference(intensity, flat_field, dark_field, correlation, blend_width, padding, cutoff):
    shift_by = correlation[0]
    blend_size = blend_width[0]
    margin = padding[0]
    limit_order = cutoff[0]
    projected = -jnp.log((intensity - dark_field) / (flat_field - dark_field))
    by_row = jnp.transpose(projected, (1, 0, 2))
    length = 4 * DET
    kept_bins = 2 * DET
    frequency = jnp.arange(kept_bins).astype(jnp.float32)
    ramp_gain = (frequency / kept_bins) * (1.0 + jnp.cos(math.pi * frequency / kept_bins))
    drop_gain = 1.0 - 1.0 / (1.0 + (frequency / FCUT) ** 8)
    orders = jnp.arange(HALF, dtype=jnp.int32)
    chosen = ((orders < limit_order) | (orders > HALF - limit_order)).astype(jnp.float32)[:, None]

    def one_row(sheet):
        stitched = stitch(sheet[:HALF], sheet[HALF:], shift_by, blend_size)
        extended = extend(stitched, margin, length)
        spectrum = jnp.fft.fft(extended, axis=-1)[:, :kept_bins]
        low_part = jnp.fft.ifft(jnp.fft.fft(spectrum, axis=0) * chosen, axis=0)
        filtered = (spectrum - drop_gain * low_part) * ramp_gain
        padded_spec = jnp.concatenate([filtered, jnp.zeros((HALF, 1), filtered.dtype)], axis=1)
        return jnp.fft.irfft(padded_spec, n=length, axis=-1)[:, :kept_bins]

    cleaned = lax.map(one_row, by_row)
    order_index = jnp.arange(HALF, dtype=jnp.int32)
    block_index = order_index // HB
    inner_index = order_index % HB
    halves = N_ANGLE // 2
    source = (block_index % halves) * 2 * HB + (block_index // halves) * HB + inner_index
    return jnp.transpose(cleaned, (1, 0, 2))[source].astype(jnp.float32)
```

```python
import functools
import math

import jax
import jax.numpy as jnp
import ml_dtypes
import numpy as np
from jax import lax
from jax.experimental import pallas as pl
from jax.experimental.pallas import tpu as pltpu
from jax.sharding import PartitionSpec as P

KMAX = 8
FCUT = 512
SIDE = 128
HALF_SIDE = SIDE // 2
QUARTER = SIDE // 4
MODES = 2 * KMAX
GROUP = 4
CHUNKS = (16, 16, 16, 16)
BF16 = jnp.bfloat16
F32 = jnp.float32


def swapped(value, axis, bit):
    mask = 2**bit
    pairs = [(source, source ^ mask) for source in range(lax.axis_size(axis))]
    return lax.ppermute(value, axis, pairs)


def np_split(table):
    high = table.astype(ml_dtypes.bfloat16)
    low = (table - high.astype(np.float64)).astype(ml_dtypes.bfloat16)
    return high, low


@functools.cache
def transform_tables():
    n = SIDE * SIDE
    a = np.arange(SIDE)
    k = np.arange(HALF_SIDE)
    angle = 2 * np.pi * (k[:, None] * a[None, :] % SIDE) / SIDE
    first = np.concatenate([np.cos(angle), -np.sin(angle)])
    first[HALF_SIDE] = 1.0 - 2.0 * (a % 2)
    first_hi, first_lo = np_split(first)
    head = slice(0, HALF_SIDE)
    tail = slice(HALF_SIDE, SIDE)
    first_pack = np.concatenate([first_hi[:, head], first_hi[:, head], first_lo[:, head]], axis=1)
    edge_pack = np.concatenate([first_hi[:, tail], first_lo[:, tail]], axis=1)
    bins = np.stack([k, np.where(k == 0, HALF_SIDE, k)]).reshape(-1)
    turn = 2 * np.pi * (bins[:, None] * a[None, :]) / n
    twiddle = np.concatenate([np.cos(turn), np.sin(turn)], axis=1).astype(np.float32)
    inner = 2 * np.pi * (a[:, None] * a[None, :] % SIDE) / SIDE
    c, s = np.cos(inner), np.sin(inner)
    forward_hi, forward_lo = np_split(np.block([[c, -s], [s, c]]))
    back_hi, back_lo = np_split(np.block([[c, s], [-s, c]]))
    forward = np.concatenate([forward_hi, forward_hi, forward_lo])
    back = np.concatenate([back_hi, back_hi, back_lo])
    f = bins[:, None] + SIDE * a[None, :]
    f = np.minimum(f, n - f).astype(np.float64)
    kept = n // 2
    ramp = f / kept * (1.0 + np.cos(np.pi * f / kept)) / n
    drop = 1.0 - 1.0 / (1.0 + (f / FCUT) ** 8)
    last = 2.0 * first[:, :HALF_SIDE].T
    last[:, 0] = 1.0
    last[:, HALF_SIDE] = 1.0 - 2.0 * (np.arange(HALF_SIDE) % 2)
    last_hi, last_lo = np_split(last)
    last_pack = np.concatenate([last_hi, last_hi, last_lo], axis=1)
    return {
        "first": first_pack,
        "edge": edge_pack,
        "twiddle": twiddle,
        "forward": forward,
        "back": back,
        "ramp": np.concatenate([ramp, ramp], axis=1).astype(np.float32),
        "ramp_drop": np.concatenate([ramp * drop, ramp * drop], axis=1).astype(np.float32),
        "last": last_pack,
    }


@functools.cache
def mode_basis(count, half_turn):
    order = np.arange(KMAX)
    angle = 2 * np.pi * (np.arange(count)[:, None] * order[None, :] % half_turn) / half_turn
    return np.concatenate([np.cos(angle), np.sin(angle)], axis=1)


def phase_rows(starts, half_turn):
    order = np.arange(KMAX)
    angle = 2 * np.pi * (np.asarray(starts)[:, None] * order[None, :] % half_turn) / half_turn
    return np.concatenate([np.cos(angle), np.sin(angle)], axis=1).astype(np.float32).reshape(-1)


def split(value):
    high = value.astype(BF16)
    low = (value - high.astype(F32)).astype(BF16)
    return high, low


def dot(left, right):
    return jnp.dot(left, right, preferred_element_type=F32)


def lanes_flipped(block):
    rows = block.shape[0]
    lane = SIDE - 1 - lax.broadcasted_iota(jnp.int32, (rows, SIDE), 1)
    turned = jnp.take_along_axis(block, lane, axis=1)
    row = rows - 1 - lax.broadcasted_iota(jnp.int32, (rows, SIDE), 0)
    return jnp.take_along_axis(turned, row, axis=0)


def flipped(sheet):
    blocks = [lanes_flipped(sheet[8 * i : 8 * i + 8]) for i in range(QUARTER // 8)]
    return jnp.concatenate(blocks[::-1], axis=0)


def swap_first_rows(upper_part, lower_part):
    row = lax.broadcasted_iota(jnp.int32, upper_part.shape, 0)
    return (
        jnp.where(row == 0, lower_part, upper_part),
        jnp.where(row == 0, upper_part, lower_part),
    )


def blend_weight(correlation, blend):
    position = (
        lax.broadcasted_iota(jnp.int32, (HALF_SIDE, SIDE), 0) * SIDE
        + lax.broadcasted_iota(jnp.int32, (HALF_SIDE, SIDE), 1)
    ).astype(F32)
    pixels = QUARTER * SIDE
    center = pixels - correlation.astype(F32) / 2.0
    return jnp.clip((position + 0.5 - center) / blend.astype(F32) + 0.5, 0.0, 1.0)


def edge_response(edge_table, padding):
    index = (
        lax.broadcasted_iota(jnp.int32, (HALF_SIDE, SIDE), 0) * SIDE
        + lax.broadcasted_iota(jnp.int32, (HALF_SIDE, SIDE), 1)
    )
    after = (index < padding).astype(F32)
    before = (index >= HALF_SIDE * SIDE - padding).astype(F32)
    boxes = jnp.concatenate([after, before], axis=1)
    boxes = jnp.concatenate([boxes, boxes], axis=0).astype(BF16)
    return dot(edge_table, boxes)


def transform_group(views, weight, correlation, edges, tables, gain, shifted, count):
    whole = correlation // SIDE
    part = correlation % SIDE
    lane = lax.broadcasted_iota(jnp.int32, (HALF_SIDE, SIDE), 1)
    in_row = lane < SIDE - part
    keep = 1.0 - weight[:QUARTER]
    stitched = []
    for i, (main, back) in enumerate(views):
        rolled = pltpu.roll(main, SIDE - part, 1)
        last = jnp.broadcast_to(main[QUARTER - 1 :, SIDE - 1 :], (QUARTER + 8, SIDE))
        shifted[i, QUARTER : 2 * QUARTER, :] = rolled
        shifted[i, 2 * QUARTER :, :] = last
        right = jnp.where(
            in_row,
            shifted[i, pl.ds(whole, HALF_SIDE), :],
            shifted[i, pl.ds(whole + 1, HALF_SIDE), :],
        )
        sheet = weight * right
        top = sheet[:QUARTER] + keep * flipped(back)
        stitched.append(jnp.concatenate([top, sheet[QUARTER:]], axis=0))
    high, low = split(jnp.concatenate(stitched, axis=1))
    grown = dot(tables["first"][...], jnp.concatenate([high, low, high], axis=0))
    after, before = edges[:, :SIDE], edges[:, SIDE:]
    cos_turn, sin_turn = tables["twiddle"][:, :SIDE], tables["twiddle"][:, SIDE:]
    real, imag = [], []
    for i, sheet in enumerate(stitched):
        ends = (
            grown[:, i * SIDE : (i + 1) * SIDE]
            + sheet[HALF_SIDE - 1 :, SIDE - 1 :] * after
            + sheet[:1, :1] * before
        )
        real.append(ends[:HALF_SIDE])
        imag.append(ends[HALF_SIDE:])
    for i in range(0, count, 2):
        imag[i], real[i + 1] = swap_first_rows(imag[i], real[i + 1])
    turned = []
    for i in range(count):
        rows = slice((i % 2) * HALF_SIDE, (i % 2 + 1) * HALF_SIDE)
        c, s = cos_turn[rows], sin_turn[rows]
        turned.append(jnp.concatenate([real[i] * c + imag[i] * s, imag[i] * c - real[i] * s], axis=1))
    high, low = split(jnp.concatenate(turned, axis=0))
    spectrum = dot(jnp.concatenate([high, low, high], axis=1), tables["forward"][...])
    gains = jnp.concatenate([gain[...]] * (count // 2), axis=0)
    high, low = split(spectrum * gains)
    inner = dot(jnp.concatenate([high, low, high], axis=1), tables["back"][...])
    real, imag = [], []
    for i in range(count):
        rows = slice((i % 2) * HALF_SIDE, (i % 2 + 1) * HALF_SIDE)
        c, s = cos_turn[rows], sin_turn[rows]
        block = inner[i * HALF_SIDE : (i + 1) * HALF_SIDE]
        real.append(block[:, :SIDE] * c - block[:, SIDE:] * s)
        imag.append(block[:, SIDE:] * c + block[:, :SIDE] * s)
    for i in range(0, count, 2):
        imag[i], real[i + 1] = swap_first_rows(imag[i], real[i + 1])
    columns = jnp.concatenate(
        [jnp.concatenate([real[i], imag[i]], axis=0) for i in range(count)], axis=1
    )
    high, low = split(columns)
    result = dot(tables["last"][...], jnp.concatenate([high, low, high], axis=0))
    return [result[:, i * SIDE : (i + 1) * SIDE] for i in range(count)]


TABLES = ("first", "edge", "twiddle", "forward", "back", "last")


def modes_kernel(halves, raw, flat, dark, phase, basis_hi, basis_lo, mine, other, total):
    step = pl.program_id(0)
    level = jnp.log(flat[...] - dark[...])
    projected = level - jnp.log(raw[...] - dark[...])
    count = raw.shape[0]
    columns = jnp.concatenate(
        [
            projected[:, 8 * i : 8 * i + 8, :].reshape(count * 8, SIDE)
            for i in range(QUARTER // 8)
        ],
        axis=1,
    )
    high, low = split(columns)
    partial = dot(basis_hi[...], high) + dot(basis_hi[...], low) + dot(basis_lo[...], high)

    @pl.when(step == 0)
    def _():
        total[...] = partial

    @pl.when(step > 0)
    def _():
        total[...] += partial

    @pl.when(step == pl.num_programs(0) - 1)
    def _():
        place = lax.axis_index("angle")
        base = (place % halves) * MODES
        odd = place % 2
        half = KMAX // 2
        for k in range(KMAX):
            c = phase[base + k]
            s = phase[base + KMAX + k]
            even_part = total[8 * k : 8 * k + 8, :]
            odd_part = total[8 * (KMAX + k) : 8 * (KMAX + k) + 8, :]
            cos_mode = even_part * c - odd_part * s
            sin_mode = odd_part * c + even_part * s
            low_half = k < half
            spot = k % half
            is_mine = (odd == 0) if low_half else (odd == 1)

            def put(ref):
                for i in range(QUARTER // 8):
                    lanes = slice(i * SIDE, (i + 1) * SIDE)
                    ref[spot, 8 * i : 8 * i + 8, :] = cos_mode[:, lanes]
                    ref[half + spot, 8 * i : 8 * i + 8, :] = sin_mode[:, lanes]

            @pl.when(is_mine)
            def _():
                put(mine)

            @pl.when(jnp.logical_not(is_mine))
            def _():
                put(other)


def filter_modes_kernel(
    halves, half_turn, mine, other_a, other_b, far_mine, far_other,
    correlation, blend, padding, cutoff, phase, *refs,
):
    names = TABLES + ("ramp_drop",)
    tables = dict(zip(names, refs))
    out_hi, out_lo, side, shifted, result = refs[len(names) :]
    place = lax.axis_index("angle")
    odd = place % 2
    upper = place // halves
    half = KMAX // 2
    side[upper, odd] = mine[...]
    side[upper, 1 - odd] = other_a[...] + other_b[...]
    side[1 - upper, odd] = far_mine[...]
    side[1 - upper, 1 - odd] = far_other[...]
    shifted[:, :QUARTER, :] = jnp.zeros((GROUP, QUARTER, SIDE), F32)
    weight = blend_weight(correlation[0], blend[0])
    edges = edge_response(tables["edge"][...], padding[0])
    for first in range(0, MODES, GROUP):
        views = [
            (side[0, m // KMAX, m % KMAX], side[1, m // KMAX, m % KMAX])
            for m in range(first, first + GROUP)
        ]
        sheets = transform_group(
            views, weight, correlation[0], edges, tables, tables["ramp_drop"], shifted, GROUP
        )
        for i, sheet in enumerate(sheets):
            result[first + i] = sheet
    base = place * MODES
    for k in range(KMAX):
        spot = (k // half) * KMAX + k % half
        scale = jnp.where(k < cutoff[0], (1.0 if k == 0 else 2.0) / half_turn, 0.0)
        c = phase[base + k] * scale
        s = phase[base + KMAX + k] * scale
        cos_sheet, sin_sheet = result[spot], result[spot + half]
        for row, sheet in (
            (k, cos_sheet * c + sin_sheet * s),
            (KMAX + k, sin_sheet * c - cos_sheet * s),
        ):
            high, low = split(sheet)
            for i in range(HALF_SIDE // 8):
                lanes = slice(i * SIDE, (i + 1) * SIDE)
                out_hi[8 * row : 8 * row + 8, lanes] = high[8 * i : 8 * i + 8]
                out_lo[8 * row : 8 * row + 8, lanes] = low[8 * i : 8 * i + 8]


def sheets_kernel(
    halves, offset, count, raw, partner, flat, dark,
    correlation, blend, padding, modes_hi, modes_lo, basis_hi, basis_lo, *refs,
):
    names = TABLES + ("ramp",)
    tables = dict(zip(names, refs))
    out, own, shifted, low, done, in_sem, out_sem = refs[-7:]
    place = lax.axis_index("angle")
    is_upper = place >= halves
    half_block = raw.shape[0] // 2
    start = jnp.where(is_upper, half_block, 0) + offset
    fetch = pltpu.make_async_copy(raw.at[pl.ds(start, count)], own, in_sem)
    fetch.start()
    shifted[:, :QUARTER, :] = jnp.zeros((GROUP, QUARTER, SIDE), F32)
    weight = blend_weight(correlation[0], blend[0])
    edges = edge_response(tables["edge"][...], padding[0])
    level = jnp.log(flat[...] - dark[...])
    low[...] = (
        dot(basis_hi[...], modes_hi[...])
        + dot(basis_hi[...], modes_lo[...])
        + dot(basis_lo[...], modes_hi[...])
    )
    fetch.wait()

    def project(sheet):
        return level - jnp.log(sheet - dark[...])

    def body(step, carry):
        first = step * GROUP
        views = []
        for i in range(GROUP):
            here, there = project(own[first + i]), project(partner[first + i])
            views.append((jnp.where(is_upper, there, here), jnp.where(is_upper, here, there)))
        sheets = transform_group(
            views, weight, correlation[0], edges, tables, tables["ramp"], shifted, GROUP
        )
        for i, sheet in enumerate(sheets):
            rows = pl.ds(pl.multiple_of((first + i) * 8, 8), 8)
            for j in range(HALF_SIDE // 8):
                done[first + i, 8 * j : 8 * j + 8, :] = (
                    sheet[8 * j : 8 * j + 8] - low[rows, j * SIDE : (j + 1) * SIDE]
                )
        return carry

    lax.fori_loop(0, count // GROUP, body, 0)
    store = pltpu.make_async_copy(done, out.at[pl.ds(offset, count)], out_sem)
    store.start()
    store.wait()


VMEM_SPEC = pl.BlockSpec(memory_space=pltpu.VMEM)
SMEM_SPEC = pl.BlockSpec(memory_space=pltpu.SMEM)
ANY_SPEC = pl.BlockSpec(memory_space=pl.ANY)
PARAMS = pltpu.CompilerParams(vmem_limit_bytes=40 * 2**20)


def partial_modes(raw, flat, dark, halves, half_turn):
    angles = raw.shape[0]
    block = 32
    steps = angles // block
    basis = mode_basis(angles, half_turn)
    spread = np.kron(basis.T, np.eye(8))
    hi, lo = np_split(spread)
    phase = phase_rows(np.arange(halves) * angles, half_turn)
    shape = jax.ShapeDtypeStruct((KMAX, QUARTER, SIDE), F32)
    whole = pl.BlockSpec((QUARTER, SIDE), lambda i: (0, 0))
    return pl.pallas_call(
        functools.partial(modes_kernel, halves),
        grid=(steps,),
        out_shape=(shape, shape),
        in_specs=[
            pl.BlockSpec((block, QUARTER, SIDE), lambda i: (i, 0, 0)),
            whole,
            whole,
            SMEM_SPEC,
            pl.BlockSpec((8 * MODES, 8 * block), lambda i: (0, i)),
            pl.BlockSpec((8 * MODES, 8 * block), lambda i: (0, i)),
        ],
        out_specs=[pl.BlockSpec((KMAX, QUARTER, SIDE), lambda i: (0, 0, 0))] * 2,
        scratch_shapes=[pltpu.VMEM((8 * MODES, QUARTER // 8 * SIDE), F32)],
        compiler_params=PARAMS,
        name="partial_modes",
    )(raw, flat, dark, jnp.asarray(phase), jnp.asarray(hi), jnp.asarray(lo))


def filtered_modes(parts, scalars, halves, half_turn, half_block):
    tables = transform_tables()
    place = np.arange(2 * halves)
    starts = place % halves * 2 * half_block + place // halves * half_block
    phase = phase_rows(starts, half_turn)
    shape = jax.ShapeDtypeStruct((8 * MODES, HALF_SIDE // 8 * SIDE), BF16)
    names = TABLES + ("ramp_drop",)
    return pl.pallas_call(
        functools.partial(filter_modes_kernel, halves, half_turn),
        out_shape=(shape, shape),
        in_specs=[VMEM_SPEC] * 5 + [SMEM_SPEC] * 5 + [VMEM_SPEC] * len(names),
        out_specs=(VMEM_SPEC, VMEM_SPEC),
        scratch_shapes=[
            pltpu.VMEM((2, 2, KMAX, QUARTER, SIDE), F32),
            pltpu.VMEM((GROUP, 3 * QUARTER + 8, SIDE), F32),
            pltpu.VMEM((MODES, HALF_SIDE, SIDE), F32),
        ],
        compiler_params=PARAMS,
        name="filtered_modes",
    )(*parts, *scalars, jnp.asarray(phase), *(jnp.asarray(tables[name]) for name in names))


def filtered_sheets(raw, partner, flat, dark, scalars, modes, out, offset, halves, half_turn):
    tables = transform_tables()
    count = partner.shape[0]
    half_block = raw.shape[0] // 2
    basis = mode_basis(half_block, half_turn)[offset : offset + count]
    hi, lo = np_split(np.kron(basis, np.eye(8)))
    names = TABLES + ("ramp",)
    operands = [raw, partner, flat, dark, *scalars, *modes, jnp.asarray(hi), jnp.asarray(lo)]
    operands += [jnp.asarray(tables[name]) for name in names]
    specs = [ANY_SPEC] + [VMEM_SPEC] * 3 + [SMEM_SPEC] * 3 + [VMEM_SPEC] * (4 + len(names))
    aliases = {}
    if out is not None:
        aliases = {len(operands): 0}
        operands.append(out)
        specs.append(ANY_SPEC)
    return pl.pallas_call(
        functools.partial(sheets_kernel, halves, offset, count),
        out_shape=jax.ShapeDtypeStruct((half_block, HALF_SIDE, SIDE), F32),
        in_specs=specs,
        out_specs=ANY_SPEC,
        scratch_shapes=[
            pltpu.VMEM((count, QUARTER, SIDE), F32),
            pltpu.VMEM((GROUP, 3 * QUARTER + 8, SIDE), F32),
            pltpu.VMEM((8 * count, HALF_SIDE // 8 * SIDE), F32),
            pltpu.VMEM((count, HALF_SIDE, SIDE), F32),
            pltpu.SemaphoreType.DMA,
            pltpu.SemaphoreType.DMA,
        ],
        input_output_aliases=aliases,
        compiler_params=PARAMS,
        name="filtered_sheets",
    )(*operands)


def local(intensity, flat_field, dark_field, correlation, blend_width, padding, cutoff):
    angle_count = lax.axis_size("angle")
    angle_place = lax.axis_index("angle")
    halves = angle_count // 2
    top_bit = angle_count.bit_length() - 2
    angles, local_rows, pixels = intensity.shape
    half_block = angles // 2
    half_turn = half_block * angle_count
    raw = intensity.reshape(angles, QUARTER, SIDE)
    flat = flat_field.reshape(QUARTER, SIDE)
    dark = dark_field.reshape(QUARTER, SIDE)
    send_from = jnp.where(angle_place >= halves, 0, half_block)
    partners = []
    offset = 0
    for count in CHUNKS:
        outgoing = lax.dynamic_slice_in_dim(raw, send_from + offset, count, 0)
        partners.append(swapped(outgoing, "angle", top_bit))
        offset += count
    mine, other = partial_modes(raw, flat, dark, halves, half_turn)
    for bit in range(1, top_bit):
        mine = mine + swapped(mine, "angle", bit)
        other = other + swapped(other, "angle", bit)
    mine_sum = mine + swapped(other, "angle", 0)
    other_more = swapped(mine, "angle", 0)
    far_mine = swapped(mine_sum, "angle", top_bit)
    far_other = swapped(far_mine, "angle", 0)
    scalars = (correlation, blend_width, padding)
    modes = filtered_modes(
        (mine_sum, other, other_more, far_mine, far_other),
        scalars + (cutoff,), halves, half_turn, half_block,
    )
    out = None
    offset = 0
    for count, partner in zip(CHUNKS, partners):
        out = filtered_sheets(
            raw, partner, flat, dark, scalars, modes, out, offset, halves, half_turn
        )
        offset += count
    return out.reshape(half_block, local_rows, 2 * pixels)


def solution(mesh):
    placed = (P("angle", "row", None), P("row", None), P("row", None), P(), P(), P(), P())
    return jax.shard_map(
        local, mesh=mesh, in_specs=placed, out_specs=P("angle", "row", None), check_vma=False
    )
```

```python
import functools
import math

import jax
import jax.numpy as jnp
import ml_dtypes
import numpy as np
from jax import lax
from jax.experimental import pallas as pl
from jax.experimental.pallas import tpu as pltpu
from jax.sharding import PartitionSpec as P

KMAX = 8
FCUT = 512
SIDE = 128
HALF_SIDE = SIDE // 2
QUARTER = SIDE // 4
MODES = 2 * KMAX
CHUNKS = ((12,), (10,), (16,), (14,), (12,))
BF16 = jnp.bfloat16
F32 = jnp.float32


def swapped(value, axis, bit):
    mask = 2**bit
    pairs = [(source, source ^ mask) for source in range(lax.axis_size(axis))]
    return lax.ppermute(value, axis, pairs)


def np_split(table):
    high = table.astype(ml_dtypes.bfloat16)
    low = (table - high.astype(np.float64)).astype(ml_dtypes.bfloat16)
    return high, low


@functools.cache
def transform_tables():
    n = SIDE * SIDE
    a = np.arange(SIDE)
    k = np.arange(HALF_SIDE)
    angle = 2 * np.pi * (k[:, None] * a[None, :] % SIDE) / SIDE
    first = np.concatenate([np.cos(angle), -np.sin(angle)])
    first[HALF_SIDE] = 1.0 - 2.0 * (a % 2)
    first_hi, first_lo = np_split(first)
    head = slice(0, HALF_SIDE)
    tail = slice(HALF_SIDE, SIDE)
    first_pack = np.concatenate([first_hi[:, head], first_hi[:, head], first_lo[:, head]], axis=1)
    edge_pack = np.concatenate([first_hi[:, tail], first_lo[:, tail]], axis=1)
    bins = np.stack([k, np.where(k == 0, HALF_SIDE, k)]).reshape(-1)
    turn = 2 * np.pi * (bins[:, None] * a[None, :]) / n
    twiddle = np.concatenate([np.cos(turn), np.sin(turn)], axis=1).astype(np.float32)
    inner = 2 * np.pi * (a[:, None] * a[None, :] % SIDE) / SIDE
    c, s = np.cos(inner), np.sin(inner)
    forward_hi, forward_lo = np_split(np.block([[c, -s], [s, c]]))
    back_hi, back_lo = np_split(np.block([[c, s], [-s, c]]))
    forward = np.concatenate([forward_hi, forward_hi, forward_lo])
    back = np.concatenate([back_hi, back_hi, back_lo])
    f = bins[:, None] + SIDE * a[None, :]
    f = np.minimum(f, n - f).astype(np.float64)
    kept = n // 2
    ramp = f / kept * (1.0 + np.cos(np.pi * f / kept)) / n
    drop = 1.0 - 1.0 / (1.0 + (f / FCUT) ** 8)
    last = 2.0 * first[:, :HALF_SIDE].T
    last[:, 0] = 1.0
    last[:, HALF_SIDE] = 1.0 - 2.0 * (np.arange(HALF_SIDE) % 2)
    last_hi, last_lo = np_split(last)
    last_pack = np.concatenate([last_hi, last_hi, last_lo], axis=1)
    return {
        "first": first_pack,
        "edge": edge_pack,
        "twiddle": twiddle,
        "forward": forward,
        "back": back,
        "ramp": np.concatenate([ramp, ramp], axis=1).astype(np.float32),
        "ramp_drop": np.concatenate([ramp * drop, ramp * drop], axis=1).astype(np.float32),
        "last": last_pack,
    }


@functools.cache
def mode_basis(count, half_turn):
    order = np.arange(KMAX)
    angle = 2 * np.pi * (np.arange(count)[:, None] * order[None, :] % half_turn) / half_turn
    return np.concatenate([np.cos(angle), np.sin(angle)], axis=1)


def phase_rows(starts, half_turn):
    order = np.arange(KMAX)
    angle = 2 * np.pi * (np.asarray(starts)[:, None] * order[None, :] % half_turn) / half_turn
    return np.concatenate([np.cos(angle), np.sin(angle)], axis=1).astype(np.float32)


def split(value):
    high = value.astype(BF16)
    low = (value - high.astype(F32)).astype(BF16)
    return high, low


def dot(left, right):
    return jnp.dot(left, right, preferred_element_type=F32)


def lanes_flipped(block):
    rows = block.shape[0]
    lane = SIDE - 1 - lax.broadcasted_iota(jnp.int32, (rows, SIDE), 1)
    turned = jnp.take_along_axis(block, lane, axis=1)
    row = rows - 1 - lax.broadcasted_iota(jnp.int32, (rows, SIDE), 0)
    return jnp.take_along_axis(turned, row, axis=0)


def flipped(sheet):
    blocks = [lanes_flipped(sheet[8 * i : 8 * i + 8]) for i in range(QUARTER // 8)]
    return jnp.concatenate(blocks[::-1], axis=0)


def swap_first_rows(upper_part, lower_part):
    row = lax.broadcasted_iota(jnp.int32, upper_part.shape, 0)
    return (
        jnp.where(row == 0, lower_part, upper_part),
        jnp.where(row == 0, upper_part, lower_part),
    )


def blend_weight(correlation, blend):
    position = (
        lax.broadcasted_iota(jnp.int32, (HALF_SIDE, SIDE), 0) * SIDE
        + lax.broadcasted_iota(jnp.int32, (HALF_SIDE, SIDE), 1)
    ).astype(F32)
    pixels = QUARTER * SIDE
    center = pixels - correlation.astype(F32) / 2.0
    return jnp.clip((position + 0.5 - center) / blend.astype(F32) + 0.5, 0.0, 1.0)


def edge_response(edge_table, padding):
    index = (
        lax.broadcasted_iota(jnp.int32, (HALF_SIDE, SIDE), 0) * SIDE
        + lax.broadcasted_iota(jnp.int32, (HALF_SIDE, SIDE), 1)
    )
    after = (index < padding).astype(F32)
    before = (index >= HALF_SIDE * SIDE - padding).astype(F32)
    boxes = jnp.concatenate([after, before], axis=1)
    boxes = jnp.concatenate([boxes, boxes], axis=0).astype(BF16)
    return dot(edge_table, boxes)


def transform_group(views, weight, correlation, edges, tables, gain, shifted, count):
    whole = correlation // SIDE
    part = correlation % SIDE
    lane = lax.broadcasted_iota(jnp.int32, (HALF_SIDE, SIDE), 1)
    in_row = lane < SIDE - part
    keep = 1.0 - weight[:QUARTER]
    stitched = []
    for i, (main, back) in enumerate(views):
        rolled = pltpu.roll(main, SIDE - part, 1)
        last = jnp.broadcast_to(main[QUARTER - 1 :, SIDE - 1 :], (QUARTER + 8, SIDE))
        shifted[i, QUARTER : 2 * QUARTER, :] = rolled
        shifted[i, 2 * QUARTER :, :] = last
        right = jnp.where(
            in_row,
            shifted[i, pl.ds(whole, HALF_SIDE), :],
            shifted[i, pl.ds(whole + 1, HALF_SIDE), :],
        )
        sheet = weight * right
        top = sheet[:QUARTER] + keep * flipped(back)
        stitched.append(jnp.concatenate([top, sheet[QUARTER:]], axis=0))
    high, low = split(jnp.concatenate(stitched, axis=1))
    grown = dot(tables["first"][...], jnp.concatenate([high, low, high], axis=0))
    after, before = edges[:, :SIDE], edges[:, SIDE:]
    cos_turn, sin_turn = tables["twiddle"][:, :SIDE], tables["twiddle"][:, SIDE:]
    real, imag = [], []
    for i, sheet in enumerate(stitched):
        ends = (
            grown[:, i * SIDE : (i + 1) * SIDE]
            + sheet[HALF_SIDE - 1 :, SIDE - 1 :] * after
            + sheet[:1, :1] * before
        )
        real.append(ends[:HALF_SIDE])
        imag.append(ends[HALF_SIDE:])
    for i in range(0, count, 2):
        imag[i], real[i + 1] = swap_first_rows(imag[i], real[i + 1])
    turned = []
    for i in range(count):
        rows = slice((i % 2) * HALF_SIDE, (i % 2 + 1) * HALF_SIDE)
        c, s = cos_turn[rows], sin_turn[rows]
        turned.append(jnp.concatenate([real[i] * c + imag[i] * s, imag[i] * c - real[i] * s], axis=1))
    high, low = split(jnp.concatenate(turned, axis=0))
    spectrum = dot(jnp.concatenate([high, low, high], axis=1), tables["forward"][...])
    gains = jnp.concatenate([gain[...]] * (count // 2), axis=0)
    high, low = split(spectrum * gains)
    inner = dot(jnp.concatenate([high, low, high], axis=1), tables["back"][...])
    real, imag = [], []
    for i in range(count):
        rows = slice((i % 2) * HALF_SIDE, (i % 2 + 1) * HALF_SIDE)
        c, s = cos_turn[rows], sin_turn[rows]
        block = inner[i * HALF_SIDE : (i + 1) * HALF_SIDE]
        real.append(block[:, :SIDE] * c - block[:, SIDE:] * s)
        imag.append(block[:, SIDE:] * c + block[:, :SIDE] * s)
    for i in range(0, count, 2):
        imag[i], real[i + 1] = swap_first_rows(imag[i], real[i + 1])
    columns = jnp.concatenate(
        [jnp.concatenate([real[i], imag[i]], axis=0) for i in range(count)], axis=1
    )
    high, low = split(columns)
    result = dot(tables["last"][...], jnp.concatenate([high, low, high], axis=0))
    return [result[:, i * SIDE : (i + 1) * SIDE] for i in range(count)]


TABLES = ("first", "edge", "twiddle", "forward", "back", "last")


def picked(place, values):
    result = jnp.float32(values[-1])
    for i, value in enumerate(values[:-1]):
        result = jnp.where(place == i, jnp.float32(value), result)
    return result


def rotations(place, starts, half_turn):
    table = phase_rows(starts, half_turn)
    cos = [picked(place, list(table[:, k])) for k in range(KMAX)]
    sin = [picked(place, list(table[:, KMAX + k])) for k in range(KMAX)]
    return cos, sin


def send_from(raw, halves):
    return jnp.where(lax.axis_index("angle") >= halves, 0, raw.shape[0] // 2)


def start_pieces(halves, offset, raw, pieces, sems):
    start = send_from(raw, halves) + offset
    copies = []
    for i, piece in enumerate(pieces):
        count = piece.shape[0]
        copies.append(pltpu.make_async_copy(raw.at[pl.ds(start, count)], piece, sems.at[i]))
        copies[-1].start()
        start = start + count
    return copies


def head_kernel(
    halves, half_turn, raw_far, flat_far, dark_far, basis_far,
    piece, mine, other, level, dark, raw, flat, basis, sems,
):
    blocks = 4
    block = raw.shape[0] // blocks
    pairs = [(flat_far, flat), (dark_far, dark), (basis_far, basis)]
    for i in range(blocks):
        rows = pl.ds(i * block, block)
        pairs.append((raw_far.at[rows], raw.at[rows]))
    start = send_from(raw, halves)
    pairs.append((raw_far.at[pl.ds(start, piece.shape[0])], piece))
    copies = [
        pltpu.make_async_copy(source, target, sems.at[i])
        for i, (source, target) in enumerate(pairs)
    ]
    for copy in copies:
        copy.start()
    copies[0].wait()
    copies[1].wait()
    level[...] = jnp.log(flat[...] - dark[...])
    turns = phase_rows(np.arange(blocks) * block, half_turn)
    cos_total, sin_total = [0.0] * KMAX, [0.0] * KMAX
    for i in range(blocks):
        copies[3 + i].wait()
        projected = level[...] - jnp.log(raw[i * block : (i + 1) * block] - dark[...])
        columns = jnp.concatenate(
            [
                projected[:, 8 * j : 8 * j + 8, :].reshape(block * 8, SIDE)
                for j in range(QUARTER // 8)
            ],
            axis=1,
        )
        high, low = split(columns)
        if i == 0:
            copies[2].wait()
        partial = dot(basis[...], jnp.concatenate([high, low, high], axis=0))
        for k in range(KMAX):
            c, s = float(turns[i, k]), float(turns[i, KMAX + k])
            cos_part = partial[8 * k : 8 * k + 8, :]
            sin_part = partial[8 * (KMAX + k) : 8 * (KMAX + k) + 8, :]
            cos_total[k] = cos_total[k] + (cos_part * c - sin_part * s)
            sin_total[k] = sin_total[k] + (sin_part * c + cos_part * s)
    place = lax.axis_index("angle")
    cos, sin = rotations(place % halves, np.arange(halves) * raw.shape[0], half_turn)
    odd = place % 2
    half = KMAX // 2
    for k in range(KMAX):
        cos_mode = cos_total[k] * cos[k] - sin_total[k] * sin[k]
        sin_mode = sin_total[k] * cos[k] + cos_total[k] * sin[k]
        spot = k % half
        is_mine = odd == k // half

        def put(ref):
            for i in range(QUARTER // 8):
                lanes = slice(i * SIDE, (i + 1) * SIDE)
                ref[spot, 8 * i : 8 * i + 8, :] = cos_mode[:, lanes]
                ref[half + spot, 8 * i : 8 * i + 8, :] = sin_mode[:, lanes]

        @pl.when(is_mine)
        def _():
            put(mine)

        @pl.when(jnp.logical_not(is_mine))
        def _():
            put(other)

    copies[-1].wait()


def add_kernel(halves, offset, raw, mine, received, total, *refs):
    pieces, sems = refs[:-1], refs[-1]
    copies = start_pieces(halves, offset, raw, pieces, sems)
    total[...] = mine[...] + received[...]
    for copy in copies:
        copy.wait()


def filter_modes(
    halves, half_turn, mine, other_a, other_b, far_mine, far_other,
    weight, correlation, edges, cutoff, starts, tables, modes, side, shifted, result,
):
    place = lax.axis_index("angle")
    odd = place % 2
    upper = place // halves
    half = KMAX // 2
    side[upper, odd] = mine[...]
    side[upper, 1 - odd] = other_a[...] + other_b[...]
    side[1 - upper, odd] = far_mine[...]
    side[1 - upper, 1 - odd] = far_other[...]
    views = [
        (side[0, m // KMAX, m % KMAX], side[1, m // KMAX, m % KMAX]) for m in range(MODES)
    ]
    sheets = transform_group(
        views, weight, correlation, edges, tables, tables["ramp_drop"], shifted, MODES
    )
    for m, sheet in enumerate(sheets):
        result[m] = sheet
    cos, sin = rotations(place, starts, half_turn)
    for k in range(KMAX):
        spot = (k // half) * KMAX + k % half
        scale = jnp.where(k < cutoff, (1.0 if k == 0 else 2.0) / half_turn, 0.0)
        c = cos[k] * scale
        s = sin[k] * scale
        cos_sheet, sin_sheet = result[spot], result[spot + half]
        for row, sheet in (
            (k, cos_sheet * c + sin_sheet * s),
            (KMAX + k, sin_sheet * c - cos_sheet * s),
        ):
            high, low = split(sheet)
            for i in range(HALF_SIDE // 8):
                lanes = slice(i * SIDE, (i + 1) * SIDE)
                for part, value in enumerate((high, low, high)):
                    place_row = part * 8 * MODES + 8 * row
                    modes[place_row : place_row + 8, lanes] = value[8 * i : 8 * i + 8]


def low_sheets(basis, modes):
    low = dot(basis, modes)

    def block(i, j):
        return low[8 * i : 8 * i + 8, j * SIDE : (j + 1) * SIDE]

    return block


def clean_rows(halves, offset, groups, raw, partner, level, dark, weight, correlation, edges, tables, shifted, emit):
    is_upper = lax.axis_index("angle") >= halves
    start = jnp.where(is_upper, raw.shape[0] // 2, 0) + offset
    first = 0
    for size in groups:
        views = []
        for i in range(first, first + size):
            here = level[...] - jnp.log(raw[start + i] - dark[...])
            there = level[...] - jnp.log(partner[i] - dark[...])
            views.append((jnp.where(is_upper, there, here), jnp.where(is_upper, here, there)))
        sheets = transform_group(
            views, weight, correlation, edges, tables, tables["ramp"], shifted, size
        )
        emit(first, sheets)
        first += size


def prepare(settings, tables, shifted):
    shifted[:, :QUARTER, :] = jnp.zeros((shifted.shape[0], QUARTER, SIDE), F32)
    weight = blend_weight(settings[0], settings[1])
    return weight, edge_response(tables["edge"][...], settings[2])


def early_kernel(
    halves, offset, next_offset, groups, waits, raw, partner, level, dark, settings, *refs,
):
    refs = refs[waits:]
    names = TABLES + ("ramp",)
    tables = dict(zip(names, refs))
    out, *pieces, shifted, sems = refs[len(names) :]
    copies = start_pieces(halves, next_offset, raw, pieces, sems)
    weight, edges = prepare(settings, tables, shifted)

    def emit(first, sheets):
        for i, sheet in enumerate(sheets):
            out[first + i] = sheet

    clean_rows(
        halves, offset, groups, raw, partner, level, dark, weight, settings[0], edges, tables, shifted, emit
    )
    for copy in copies:
        copy.wait()


def middle_kernel(
    halves, half_turn, starts, early_count, mine, other_a, other_b, far_mine, far_other, basis,
    settings, *refs,
):
    names = TABLES + ("ramp_drop",)
    early, refs = refs[:early_count], refs[early_count:]
    tables = dict(zip(names, refs))
    fixed, modes, side, shifted, result = refs[len(names) :]
    weight, edges = prepare(settings, tables, shifted)
    filter_modes(
        halves, half_turn, mine, other_a, other_b, far_mine, far_other,
        weight, settings[0], edges, settings[3], starts, tables, modes, side, shifted, result,
    )
    low = low_sheets(basis[...], modes[...])
    row = 0
    for part in early:
        for i in range(part.shape[0]):
            for j in range(HALF_SIDE // 8):
                fixed[row, 8 * j : 8 * j + 8, :] = part[i, 8 * j : 8 * j + 8, :] - low(row, j)
            row += 1


def late_kernel(halves, offset, groups, raw, partner, level, dark, modes, basis, settings, *refs):
    names = TABLES + ("ramp",)
    tables = dict(zip(names, refs))
    *finished, out, shifted, done, sems = refs[len(names) :]
    copies = []

    def send(source, target):
        copies.append(pltpu.make_async_copy(source, target, sems.at[len(copies)]))
        copies[-1].start()

    row = 0
    for part in finished:
        send(part, out.at[pl.ds(row, part.shape[0])])
        row += part.shape[0]
    weight, edges = prepare(settings, tables, shifted)
    low = low_sheets(basis[...], modes[...])
    target = done if finished else out

    def emit(first, sheets):
        for i, sheet in enumerate(sheets):
            for j in range(HALF_SIDE // 8):
                target[first + i, 8 * j : 8 * j + 8, :] = sheet[8 * j : 8 * j + 8] - low(first + i, j)
        if finished:
            send(done.at[pl.ds(first, len(sheets))], out.at[pl.ds(offset + first, len(sheets))])

    clean_rows(
        halves, offset, groups, raw, partner, level, dark, weight, settings[0], edges, tables, shifted, emit
    )
    for copy in copies:
        copy.wait()


VMEM_SPEC = pl.BlockSpec(memory_space=pltpu.VMEM)
SMEM_SPEC = pl.BlockSpec(memory_space=pltpu.SMEM)
ANY_SPEC = pl.BlockSpec(memory_space=pl.ANY)
MIB = 2**20
COST = pl.CostEstimate(flops=0, bytes_accessed=0, transcendentals=0)


def call(kernel, name, operands, out_shape, out_specs, scratch, limit=32 * MIB):
    specs = [spec for spec, _ in operands]
    return pl.pallas_call(
        kernel,
        out_shape=out_shape,
        in_specs=specs,
        out_specs=out_specs,
        scratch_shapes=scratch,
        compiler_params=pltpu.CompilerParams(vmem_limit_bytes=limit),
        cost_estimate=COST,
        name=name,
    )(*(value for _, value in operands))


def vmem(*values):
    return [(VMEM_SPEC, jnp.asarray(value)) for value in values]


def smem(*values):
    return [(SMEM_SPEC, jnp.asarray(value)) for value in values]


def table_operands(*extra):
    tables = transform_tables()
    return vmem(*(tables[name] for name in TABLES + extra))


def shifted_scratch(count):
    return pltpu.VMEM((count, 3 * QUARTER + 8, SIDE), F32)


def sheet_scratch(count):
    return pltpu.VMEM((count, HALF_SIDE, SIDE), F32)


def basis_pack(offset, count, half_turn):
    basis = np.kron(mode_basis(offset + count, half_turn)[offset:], np.eye(8))
    hi, lo = np_split(basis)
    return np.concatenate([hi, hi, lo], axis=1)


def far(*values):
    return [
        (ANY_SPEC, pltpu.with_memory_space_constraint(jnp.asarray(value), pltpu.HBM))
        for value in values
    ]


def piece_shapes(raw, counts):
    return [jax.ShapeDtypeStruct((count,) + raw.shape[1:], F32) for count in counts]


def head(raw, flat, dark, count, halves, half_turn):
    block = raw.shape[0] // 4
    hi, lo = np_split(np.kron(mode_basis(block, half_turn).T, np.eye(8)))
    basis = np.concatenate([hi, hi, lo], axis=1)
    shapes = piece_shapes(raw, [count])
    shapes += [jax.ShapeDtypeStruct((KMAX, QUARTER, SIDE), F32)] * 2
    shapes += [jax.ShapeDtypeStruct((QUARTER, SIDE), F32)] * 2
    return call(
        functools.partial(head_kernel, halves, half_turn), "head",
        far(raw, flat, dark, basis), shapes, [VMEM_SPEC] * len(shapes),
        [
            pltpu.VMEM(raw.shape, F32),
            pltpu.VMEM(flat.shape, F32),
            pltpu.VMEM(basis.shape, BF16),
            pltpu.SemaphoreType.DMA((8,)),
        ],
    )


def add_modes(raw, mine, received, counts, offset, halves):
    shapes = [jax.ShapeDtypeStruct(mine.shape, F32)] + piece_shapes(raw, counts)
    return call(
        functools.partial(add_kernel, halves, offset), "add_modes", vmem(raw, mine, received),
        shapes, [VMEM_SPEC] * len(shapes), [pltpu.SemaphoreType.DMA((len(counts),))],
    )


def early_sheets(raw, partner, level, dark, after, settings, groups, offset, counts, next_offset, halves):
    operands = vmem(raw, partner, level, dark) + smem(settings)
    operands += [(ANY_SPEC, value) for value in after] + table_operands("ramp")
    shapes = [jax.ShapeDtypeStruct((sum(groups), HALF_SIDE, SIDE), F32)] + piece_shapes(raw, counts)
    return call(
        functools.partial(early_kernel, halves, offset, next_offset, groups, len(after)), "early_sheets",
        operands, shapes, [VMEM_SPEC] * len(shapes),
        [shifted_scratch(max(groups)), pltpu.SemaphoreType.DMA((max(len(counts), 1),))],
    )


def middle_sheets(early, parts, settings, halves, half_turn, half_block):
    count = sum(part.shape[0] for part in early)
    place = np.arange(2 * halves)
    starts = place % halves * 2 * half_block + place // halves * half_block
    operands = vmem(*parts, basis_pack(0, count, half_turn)) + smem(settings)
    operands += vmem(*early) + table_operands("ramp_drop")
    return call(
        functools.partial(middle_kernel, halves, half_turn, starts, len(early)), "middle_sheets", operands,
        (
            jax.ShapeDtypeStruct((count, HALF_SIDE, SIDE), F32),
            jax.ShapeDtypeStruct((3 * 8 * MODES, HALF_SIDE // 8 * SIDE), BF16),
        ),
        (VMEM_SPEC, VMEM_SPEC),
        [
            pltpu.VMEM((2, 2, KMAX, QUARTER, SIDE), F32),
            shifted_scratch(MODES),
            sheet_scratch(MODES),
        ],
    )


def late_sheets(raw, partner, level, dark, modes, settings, groups, offset, halves, half_turn, finished=()):
    count = sum(groups)
    operands = vmem(raw, partner, level, dark, modes, basis_pack(offset, count, half_turn))
    operands += smem(settings) + table_operands("ramp") + vmem(*finished)
    total = raw.shape[0] // 2 if finished else count
    return call(
        functools.partial(late_kernel, halves, offset, groups), "late_sheets", operands,
        jax.ShapeDtypeStruct((total, HALF_SIDE, SIDE), F32),
        ANY_SPEC if finished else VMEM_SPEC,
        [
            shifted_scratch(max(groups)),
            sheet_scratch(count),
            pltpu.SemaphoreType.DMA((len(finished) + len(groups),)),
        ],
    )


def local(intensity, flat_field, dark_field, correlation, blend_width, padding, cutoff):
    angle_count = lax.axis_size("angle")
    halves = angle_count // 2
    top_bit = angle_count.bit_length() - 2
    angles, local_rows, pixels = intensity.shape
    half_block = angles // 2
    half_turn = half_block * angle_count
    counts = [sum(groups) for groups in CHUNKS]
    starts = [sum(counts[:i]) for i in range(len(counts))]
    raw = intensity.reshape(angles, QUARTER, SIDE)
    piece, mine, other, level, dark = head(
        raw, flat_field.reshape(QUARTER, SIDE), dark_field.reshape(QUARTER, SIDE),
        counts[0], halves, half_turn,
    )
    settings = jnp.concatenate([correlation, blend_width, padding, cutoff])
    partners = [swapped(piece, "angle", top_bit)]
    for bit in range(1, top_bit):
        mine = mine + swapped(mine, "angle", bit)
        other = other + swapped(other, "angle", bit)
    received = swapped(other, "angle", 0)
    other_more = swapped(mine, "angle", 0)
    mine_sum, piece = add_modes(raw, mine, received, counts[1:2], starts[1], halves)
    partners.append(swapped(piece, "angle", top_bit))
    far_mine = swapped(mine_sum, "angle", top_bit)
    first, *pieces = early_sheets(
        raw, partners[0], level, dark, (mine_sum, other_more), settings, CHUNKS[0], 0,
        counts[2:4], starts[2], halves,
    )
    partners += [swapped(piece, "angle", top_bit) for piece in pieces]
    far_other = swapped(far_mine, "angle", 0)
    second, *pieces = early_sheets(
        raw, partners[1], level, dark, (far_mine, first), settings, CHUNKS[1], starts[1],
        counts[4:], starts[4] if len(starts) > 4 else 0, halves,
    )
    partners += [swapped(piece, "angle", top_bit) for piece in pieces]
    early = [first, second]
    parts = (mine_sum, other, other_more, far_mine, far_other)
    fixed, modes = middle_sheets(early, parts, settings, halves, half_turn, half_block)
    finished = [fixed]
    for i in range(2, len(CHUNKS)):
        finished.append(
            late_sheets(
                raw, partners[i], level, dark, modes, settings, CHUNKS[i], starts[i],
                halves, half_turn, finished if i == len(CHUNKS) - 1 else (),
            )
        )
    return finished[-1].reshape(half_block, local_rows, 2 * pixels)


def solution(mesh):
    placed = (P("angle", "row", None), P("row", None), P("row", None), P(), P(), P(), P())
    return jax.shard_map(
        local, mesh=mesh, in_specs=placed, out_specs=P("angle", "row", None), check_vma=False
    )
```

```python
import functools
import math

import jax
import jax.numpy as jnp
import ml_dtypes
import numpy as np
from jax import lax
from jax.experimental import pallas as pl
from jax.experimental.pallas import tpu as pltpu
from jax.sharding import PartitionSpec as P

KMAX = 8
FCUT = 512
SIDE = 128
HALF_SIDE = SIDE // 2
QUARTER = SIDE // 4
MODES = 2 * KMAX
MODE_GROUP = 8
CHUNKS = ((8,8,8),(6,4),(6,6),(6,4),(4,4))
BF16 = jnp.bfloat16
F32 = jnp.float32


def swapped(value, axis, bit):
    mask = 2**bit
    pairs = [(source, source ^ mask) for source in range(lax.axis_size(axis))]
    return lax.ppermute(value, axis, pairs)


def np_split(table):
    high = table.astype(ml_dtypes.bfloat16)
    low = (table - high.astype(np.float64)).astype(ml_dtypes.bfloat16)
    return high, low


@functools.cache
def transform_tables():
    n = SIDE * SIDE
    a = np.arange(SIDE)
    k = np.arange(HALF_SIDE)
    angle = 2 * np.pi * (k[:, None] * a[None, :] % SIDE) / SIDE
    first = np.concatenate([np.cos(angle), -np.sin(angle)])
    first[HALF_SIDE] = 1.0 - 2.0 * (a % 2)
    first_hi, first_lo = np_split(first)
    head = slice(0, HALF_SIDE)
    tail = slice(HALF_SIDE, SIDE)
    first_pack = np.concatenate([first_hi[:, head], first_hi[:, head], first_lo[:, head]], axis=1)
    edge_pack = np.concatenate([first_hi[:, tail], first_lo[:, tail]], axis=1)
    bins = np.stack([k, np.where(k == 0, HALF_SIDE, k)]).reshape(-1)
    turn = 2 * np.pi * (bins[:, None] * a[None, :]) / n
    twiddle = np.concatenate([np.cos(turn), np.sin(turn)], axis=1).astype(np.float32)
    inner = 2 * np.pi * (a[:, None] * a[None, :] % SIDE) / SIDE
    c, s = np.cos(inner), np.sin(inner)
    forward_hi, forward_lo = np_split(np.block([[c, -s], [s, c]]))
    back_hi, back_lo = np_split(np.block([[c, s], [-s, c]]))
    forward = np.concatenate([forward_hi, forward_hi, forward_lo])
    back = np.concatenate([back_hi, back_hi, back_lo])
    f = bins[:, None] + SIDE * a[None, :]
    f = np.minimum(f, n - f).astype(np.float64)
    kept = n // 2
    ramp = f / kept * (1.0 + np.cos(np.pi * f / kept)) / n
    drop = 1.0 - 1.0 / (1.0 + (f / FCUT) ** 8)
    last = 2.0 * first[:, :HALF_SIDE].T
    last[:, 0] = 1.0
    last[:, HALF_SIDE] = 1.0 - 2.0 * (np.arange(HALF_SIDE) % 2)
    last_hi, last_lo = np_split(last)
    last_pack = np.concatenate([last_hi, last_hi, last_lo], axis=1)
    return {
        "first": first_pack,
        "edge": edge_pack,
        "twiddle": twiddle,
        "forward": forward,
        "back": back,
        "ramp": np.concatenate([ramp, ramp], axis=1).astype(np.float32),
        "ramp_drop": np.concatenate([ramp * drop, ramp * drop], axis=1).astype(np.float32),
        "last": last_pack,
    }


@functools.cache
def mode_basis(count, half_turn):
    order = np.arange(KMAX)
    angle = 2 * np.pi * (np.arange(count)[:, None] * order[None, :] % half_turn) / half_turn
    return np.concatenate([np.cos(angle), np.sin(angle)], axis=1)


def phase_rows(starts, half_turn):
    order = np.arange(KMAX)
    angle = 2 * np.pi * (np.asarray(starts)[:, None] * order[None, :] % half_turn) / half_turn
    return np.concatenate([np.cos(angle), np.sin(angle)], axis=1).astype(np.float32)


def split(value):
    high = value.astype(BF16)
    low = (value - high.astype(F32)).astype(BF16)
    return high, low


def dot(left, right):
    return jnp.dot(left, right, preferred_element_type=F32)


def lanes_flipped(block):
    rows = block.shape[0]
    lane = SIDE - 1 - lax.broadcasted_iota(jnp.int32, (rows, SIDE), 1)
    turned = jnp.take_along_axis(block, lane, axis=1)
    row = rows - 1 - lax.broadcasted_iota(jnp.int32, (rows, SIDE), 0)
    return jnp.take_along_axis(turned, row, axis=0)


def flipped(sheet):
    blocks = [lanes_flipped(sheet[8 * i : 8 * i + 8]) for i in range(QUARTER // 8)]
    return jnp.concatenate(blocks[::-1], axis=0)


def swap_first_rows(upper_part, lower_part):
    row = lax.broadcasted_iota(jnp.int32, upper_part.shape, 0)
    return (
        jnp.where(row == 0, lower_part, upper_part),
        jnp.where(row == 0, upper_part, lower_part),
    )


def blend_weight(correlation, blend):
    position = (
        lax.broadcasted_iota(jnp.int32, (HALF_SIDE, SIDE), 0) * SIDE
        + lax.broadcasted_iota(jnp.int32, (HALF_SIDE, SIDE), 1)
    ).astype(F32)
    pixels = QUARTER * SIDE
    center = pixels - correlation.astype(F32) / 2.0
    return jnp.clip((position + 0.5 - center) / blend.astype(F32) + 0.5, 0.0, 1.0)


def edge_response(edge_table, padding):
    index = (
        lax.broadcasted_iota(jnp.int32, (HALF_SIDE, SIDE), 0) * SIDE
        + lax.broadcasted_iota(jnp.int32, (HALF_SIDE, SIDE), 1)
    )
    after = (index < padding).astype(F32)
    before = (index >= HALF_SIDE * SIDE - padding).astype(F32)
    boxes = jnp.concatenate([after, before], axis=1)
    boxes = jnp.concatenate([boxes, boxes], axis=0).astype(BF16)
    return dot(edge_table, boxes)


def transform_group(views, weight, correlation, edges, tables, gain, shifted, base, emit):
    count = len(views)
    whole = correlation // SIDE
    part = correlation % SIDE
    lane = lax.broadcasted_iota(jnp.int32, (HALF_SIDE, SIDE), 1)
    in_row = lane < SIDE - part
    keep = 1.0 - weight[:QUARTER]
    stitched = []
    for i, view in enumerate(views):
        main, back = view()
        rolled = pltpu.roll(main, SIDE - part, 1)
        last = jnp.broadcast_to(main[QUARTER - 1 :, SIDE - 1 :], (QUARTER + 8, SIDE))
        shifted[base + i, QUARTER : 2 * QUARTER, :] = rolled
        shifted[base + i, 2 * QUARTER :, :] = last
        right = jnp.where(
            in_row,
            shifted[base + i, pl.ds(whole, HALF_SIDE), :],
            shifted[base + i, pl.ds(whole + 1, HALF_SIDE), :],
        )
        sheet = weight * right
        top = sheet[:QUARTER] + keep * flipped(back)
        stitched.append(jnp.concatenate([top, sheet[QUARTER:]], axis=0))
    high, low = split(jnp.concatenate(stitched, axis=1))
    grown = dot(tables["first"][...], jnp.concatenate([high, low, high], axis=0))
    yield
    after, before = edges[:, :SIDE], edges[:, SIDE:]
    cos_turn, sin_turn = tables["twiddle"][:, :SIDE], tables["twiddle"][:, SIDE:]
    real, imag = [], []
    for i, sheet in enumerate(stitched):
        ends = (
            grown[:, i * SIDE : (i + 1) * SIDE]
            + sheet[HALF_SIDE - 1 :, SIDE - 1 :] * after
            + sheet[:1, :1] * before
        )
        real.append(ends[:HALF_SIDE])
        imag.append(ends[HALF_SIDE:])
    for i in range(0, count, 2):
        imag[i], real[i + 1] = swap_first_rows(imag[i], real[i + 1])
    turned = []
    for i in range(count):
        rows = slice((i % 2) * HALF_SIDE, (i % 2 + 1) * HALF_SIDE)
        c, s = cos_turn[rows], sin_turn[rows]
        turned.append(jnp.concatenate([real[i] * c + imag[i] * s, imag[i] * c - real[i] * s], axis=1))
    high, low = split(jnp.concatenate(turned, axis=0))
    spectrum = dot(jnp.concatenate([high, low, high], axis=1), tables["forward"][...])
    yield
    gains = jnp.concatenate([gain[...]] * (count // 2), axis=0)
    high, low = split(spectrum * gains)
    inner = dot(jnp.concatenate([high, low, high], axis=1), tables["back"][...])
    yield
    real, imag = [], []
    for i in range(count):
        rows = slice((i % 2) * HALF_SIDE, (i % 2 + 1) * HALF_SIDE)
        c, s = cos_turn[rows], sin_turn[rows]
        block = inner[i * HALF_SIDE : (i + 1) * HALF_SIDE]
        real.append(block[:, :SIDE] * c - block[:, SIDE:] * s)
        imag.append(block[:, SIDE:] * c + block[:, :SIDE] * s)
    for i in range(0, count, 2):
        imag[i], real[i + 1] = swap_first_rows(imag[i], real[i + 1])
    columns = jnp.concatenate(
        [jnp.concatenate([real[i], imag[i]], axis=0) for i in range(count)], axis=1
    )
    high, low = split(columns)
    result = dot(tables["last"][...], jnp.concatenate([high, low, high], axis=0))
    yield
    emit(base, [result[:, i * SIDE : (i + 1) * SIDE] for i in range(count)])


def take_turns(groups):
    groups = list(groups)
    while groups:
        for group in list(groups):
            if next(group, groups) is groups:
                groups.remove(group)


TABLES = ("first", "edge", "twiddle", "forward", "back", "last")


def picked(place, values):
    result = jnp.float32(values[-1])
    for i, value in enumerate(values[:-1]):
        result = jnp.where(place == i, jnp.float32(value), result)
    return result


def rotations(place, starts, half_turn):
    table = phase_rows(starts, half_turn)
    cos = [picked(place, list(table[:, k])) for k in range(KMAX)]
    sin = [picked(place, list(table[:, KMAX + k])) for k in range(KMAX)]
    return cos, sin


def send_from(raw, halves):
    return jnp.where(lax.axis_index("angle") >= halves, 0, raw.shape[0] // 2)


def start_pieces(halves, offset, raw, pieces, sems):
    start = send_from(raw, halves) + offset
    copies = []
    for i, piece in enumerate(pieces):
        count = piece.shape[0]
        copies.append(pltpu.make_async_copy(raw.at[pl.ds(start, count)], piece, sems.at[i]))
        copies[-1].start()
        start = start + count
    return copies


def head_kernel(
    halves, half_turn, raw_far, flat_far, dark_far, basis_far,
    mine, other, level, dark, raw, flat, basis, sems,
):
    blocks = 4
    block = raw.shape[0] // blocks
    pairs = [(flat_far, flat), (dark_far, dark), (basis_far, basis)]
    for i in range(blocks):
        rows = pl.ds(i * block, block)
        pairs.append((raw_far.at[rows], raw.at[rows]))
    copies = [
        pltpu.make_async_copy(source, target, sems.at[i])
        for i, (source, target) in enumerate(pairs)
    ]
    for copy in copies:
        copy.start()
    copies[0].wait()
    copies[1].wait()
    level[...] = jnp.log(flat[...] - dark[...])
    turns = phase_rows(np.arange(blocks) * block, half_turn)
    cos_total, sin_total = [0.0] * KMAX, [0.0] * KMAX
    for i in range(blocks):
        copies[3 + i].wait()
        projected = level[...] - jnp.log(raw[i * block : (i + 1) * block] - dark[...])
        columns = jnp.concatenate(
            [
                projected[:, 8 * j : 8 * j + 8, :].reshape(block * 8, SIDE)
                for j in range(QUARTER // 8)
            ],
            axis=1,
        )
        high, low = split(columns)
        if i == 0:
            copies[2].wait()
        partial = dot(basis[...], jnp.concatenate([high, low, high], axis=0))
        for k in range(KMAX):
            c, s = float(turns[i, k]), float(turns[i, KMAX + k])
            cos_part = partial[8 * k : 8 * k + 8, :]
            sin_part = partial[8 * (KMAX + k) : 8 * (KMAX + k) + 8, :]
            cos_total[k] = cos_total[k] + (cos_part * c - sin_part * s)
            sin_total[k] = sin_total[k] + (sin_part * c + cos_part * s)
    place = lax.axis_index("angle")
    cos, sin = rotations(place % halves, np.arange(halves) * raw.shape[0], half_turn)
    odd = place % 2
    half = KMAX // 2
    for k in range(KMAX):
        cos_mode = cos_total[k] * cos[k] - sin_total[k] * sin[k]
        sin_mode = sin_total[k] * cos[k] + cos_total[k] * sin[k]
        spot = k % half
        is_mine = odd == k // half

        def put(ref):
            for i in range(QUARTER // 8):
                lanes = slice(i * SIDE, (i + 1) * SIDE)
                ref[spot, 8 * i : 8 * i + 8, :] = cos_mode[:, lanes]
                ref[half + spot, 8 * i : 8 * i + 8, :] = sin_mode[:, lanes]

        @pl.when(is_mine)
        def _():
            put(mine)

        @pl.when(jnp.logical_not(is_mine))
        def _():
            put(other)


def piece_kernel(halves, raw_far, piece, sems):
    start_pieces(halves, 0, raw_far, [piece], sems)[0].wait()


def add_kernel(halves, offset, raw, mine, received, total, *refs):
    pieces, sems = refs[:-1], refs[-1]
    copies = start_pieces(halves, offset, raw, pieces, sems)
    total[...] = mine[...] + received[...]
    for copy in copies:
        copy.wait()


def filter_modes(
    halves, half_turn, mine, other_a, other_b, far_mine, far_other,
    weight, correlation, edges, cutoff, starts, tables, modes, side, shifted, result,
):
    place = lax.axis_index("angle")
    odd = place % 2
    upper = place // halves
    half = KMAX // 2
    side[upper, odd] = mine[...]
    side[upper, 1 - odd] = other_a[...] + other_b[...]
    side[1 - upper, odd] = far_mine[...]
    side[1 - upper, 1 - odd] = far_other[...]

    def view(m):
        return lambda: (side[0, m // KMAX, m % KMAX], side[1, m // KMAX, m % KMAX])

    def emit(first, sheets):
        for i, sheet in enumerate(sheets):
            result[first + i] = sheet

    take_turns(
        transform_group(
            [view(m) for m in range(first, first + MODE_GROUP)],
            weight, correlation, edges, tables, tables["ramp_drop"], shifted, first, emit,
        )
        for first in range(0, MODES, MODE_GROUP)
    )
    cos, sin = rotations(place, starts, half_turn)
    for k in range(KMAX):
        spot = (k // half) * KMAX + k % half
        scale = jnp.where(k < cutoff, (1.0 if k == 0 else 2.0) / half_turn, 0.0)
        c = cos[k] * scale
        s = sin[k] * scale
        cos_sheet, sin_sheet = result[spot], result[spot + half]
        for row, sheet in (
            (k, cos_sheet * c + sin_sheet * s),
            (KMAX + k, sin_sheet * c - cos_sheet * s),
        ):
            high, low = split(sheet)
            for i in range(HALF_SIDE // 8):
                lanes = slice(i * SIDE, (i + 1) * SIDE)
                for part, value in enumerate((high, low, high)):
                    place_row = part * 8 * MODES + 8 * row
                    modes[place_row : place_row + 8, lanes] = value[8 * i : 8 * i + 8]


def low_sheets(basis, modes):
    low = dot(basis, modes)

    def block(i, j):
        return low[8 * i : 8 * i + 8, j * SIDE : (j + 1) * SIDE]

    return block


def clean_rows(halves, offset, groups, raw, partner, level, dark, weight, correlation, edges, tables, shifted, emit):
    is_upper = lax.axis_index("angle") >= halves
    start = jnp.where(is_upper, raw.shape[0] // 2, 0) + offset

    def view(i):
        def load():
            here = level[...] - jnp.log(raw[start + i] - dark[...])
            there = level[...] - jnp.log(partner[i] - dark[...])
            return jnp.where(is_upper, there, here), jnp.where(is_upper, here, there)

        return load

    firsts = [sum(groups[:i]) for i in range(len(groups))]
    take_turns(
        transform_group(
            [view(i) for i in range(first, first + size)],
            weight, correlation, edges, tables, tables["ramp"], shifted, first, emit,
        )
        for first, size in zip(firsts, groups)
    )


def prepare(settings, tables, shifted):
    shifted[:, :QUARTER, :] = jnp.zeros((shifted.shape[0], QUARTER, SIDE), F32)
    weight = blend_weight(settings[0], settings[1])
    return weight, edge_response(tables["edge"][...], settings[2])


def early_kernel(
    halves, offset, next_offset, groups, waits, raw, partner, level, dark, settings, *refs,
):
    refs = refs[waits:]
    names = TABLES + ("ramp",)
    tables = dict(zip(names, refs))
    out, *pieces, shifted, sems = refs[len(names) :]
    copies = start_pieces(halves, next_offset, raw, pieces, sems)
    weight, edges = prepare(settings, tables, shifted)

    def emit(first, sheets):
        for i, sheet in enumerate(sheets):
            out[first + i] = sheet

    clean_rows(
        halves, offset, groups, raw, partner, level, dark, weight, settings[0], edges, tables, shifted, emit
    )
    for copy in copies:
        copy.wait()


def middle_kernel(
    halves, half_turn, starts, early_count, mine, other_a, other_b, far_mine, far_other, basis,
    settings, *refs,
):
    names = TABLES + ("ramp_drop",)
    early, refs = refs[:early_count], refs[early_count:]
    tables = dict(zip(names, refs))
    fixed, modes, side, shifted, result = refs[len(names) :]
    weight, edges = prepare(settings, tables, shifted)
    filter_modes(
        halves, half_turn, mine, other_a, other_b, far_mine, far_other,
        weight, settings[0], edges, settings[3], starts, tables, modes, side, shifted, result,
    )
    low = low_sheets(basis[...], modes[...])
    row = 0
    for part in early:
        for i in range(part.shape[0]):
            for j in range(HALF_SIDE // 8):
                fixed[row, 8 * j : 8 * j + 8, :] = part[i, 8 * j : 8 * j + 8, :] - low(row, j)
            row += 1


class Joined:
    def __init__(self, refs):
        self.rows = [(ref, i) for ref in refs for i in range(ref.shape[0])]

    def __getitem__(self, row):
        ref, i = self.rows[row]
        return ref[i]


def late_kernel(
    halves, offset, groups, writes, finished_count, partner_count, raw, level, dark, modes, basis, settings, *refs,
):
    names = TABLES + ("ramp",)
    partner, refs = Joined(refs[:partner_count]), refs[partner_count:]
    tables = dict(zip(names, refs))
    finished = refs[len(names) : len(names) + finished_count]
    out, shifted, done, sems = refs[-4:]
    copies = []

    def send(source, target):
        copies.append(pltpu.make_async_copy(source, target, sems.at[len(copies)]))
        copies[-1].start()

    row = 0
    if writes == "all":
        for part in finished:
            send(part, out.at[pl.ds(row, part.shape[0])])
            row += part.shape[0]
    weight, edges = prepare(settings, tables, shifted)
    low = low_sheets(basis[...], modes[...])
    target = done if writes else out

    def emit(first, sheets):
        for i, sheet in enumerate(sheets):
            for j in range(HALF_SIDE // 8):
                target[first + i, 8 * j : 8 * j + 8, :] = sheet[8 * j : 8 * j + 8] - low(first + i, j)
        if writes:
            send(done.at[pl.ds(first, len(sheets))], out.at[pl.ds(offset + first, len(sheets))])

    clean_rows(
        halves, offset, groups, raw, partner, level, dark, weight, settings[0], edges, tables, shifted, emit
    )
    for copy in copies:
        copy.wait()


VMEM_SPEC = pl.BlockSpec(memory_space=pltpu.VMEM)
SMEM_SPEC = pl.BlockSpec(memory_space=pltpu.SMEM)
ANY_SPEC = pl.BlockSpec(memory_space=pl.ANY)
MIB = 2**20
HEAD_COST = 16 * MIB


def call(kernel, name, operands, out_shape, out_specs, scratch, limit=32 * MIB, aliases=(), cost=0):
    specs = [spec for spec, _ in operands]
    return pl.pallas_call(
        kernel,
        out_shape=out_shape,
        in_specs=specs,
        out_specs=out_specs,
        scratch_shapes=scratch,
        input_output_aliases=dict(aliases),
        compiler_params=pltpu.CompilerParams(vmem_limit_bytes=limit),
        cost_estimate=pl.CostEstimate(flops=0, bytes_accessed=cost, transcendentals=0),
        name=name,
    )(*(value for _, value in operands))


def vmem(*values):
    return [(VMEM_SPEC, jnp.asarray(value)) for value in values]


def smem(*values):
    return [(SMEM_SPEC, jnp.asarray(value)) for value in values]


def table_operands(*extra):
    tables = transform_tables()
    return vmem(*(tables[name] for name in TABLES + extra))


def shifted_scratch(count):
    return pltpu.VMEM((count, 3 * QUARTER + 8, SIDE), F32)


def sheet_scratch(count):
    return pltpu.VMEM((count, HALF_SIDE, SIDE), F32)


def basis_pack(offset, count, half_turn):
    basis = np.kron(mode_basis(offset + count, half_turn)[offset:], np.eye(8))
    hi, lo = np_split(basis)
    return np.concatenate([hi, hi, lo], axis=1)


def far(*values):
    return [
        (ANY_SPEC, pltpu.with_memory_space_constraint(jnp.asarray(value), pltpu.HBM))
        for value in values
    ]


def piece_shapes(raw, counts):
    return [jax.ShapeDtypeStruct((count,) + raw.shape[1:], F32) for count in counts]


def head(raw, flat, dark, halves, half_turn):
    block = raw.shape[0] // 4
    hi, lo = np_split(np.kron(mode_basis(block, half_turn).T, np.eye(8)))
    basis = np.concatenate([hi, hi, lo], axis=1)
    shapes = [jax.ShapeDtypeStruct((KMAX, QUARTER, SIDE), F32)] * 2
    shapes += [jax.ShapeDtypeStruct((QUARTER, SIDE), F32)] * 2
    return call(
        functools.partial(head_kernel, halves, half_turn), "head",
        far(raw, flat, dark, basis), shapes, [VMEM_SPEC] * len(shapes),
        [
            pltpu.VMEM(raw.shape, F32),
            pltpu.VMEM(flat.shape, F32),
            pltpu.VMEM(basis.shape, BF16),
            pltpu.SemaphoreType.DMA((7,)),
        ],
        cost=HEAD_COST,
    )


def first_piece(raw, count, halves):
    return call(
        functools.partial(piece_kernel, halves), "first_piece", far(raw),
        piece_shapes(raw, [count])[0], VMEM_SPEC, [pltpu.SemaphoreType.DMA((1,))],
    )


def add_modes(raw, mine, received, counts, offset, halves):
    shapes = [jax.ShapeDtypeStruct(mine.shape, F32)] + piece_shapes(raw, counts)
    return call(
        functools.partial(add_kernel, halves, offset), "add_modes", vmem(raw, mine, received),
        shapes, [VMEM_SPEC] * len(shapes), [pltpu.SemaphoreType.DMA((len(counts),))],
    )


def early_sheets(raw, partner, level, dark, after, settings, groups, offset, counts, next_offset, halves):
    operands = vmem(raw, partner, level, dark) + smem(settings)
    operands += [(ANY_SPEC, value) for value in after] + table_operands("ramp")
    shapes = [jax.ShapeDtypeStruct((sum(groups), HALF_SIDE, SIDE), F32)] + piece_shapes(raw, counts)
    return call(
        functools.partial(early_kernel, halves, offset, next_offset, groups, len(after)), "early_sheets",
        operands, shapes, [VMEM_SPEC] * len(shapes),
        [shifted_scratch(sum(groups)), pltpu.SemaphoreType.DMA((max(len(counts), 1),))],
    )


def middle_sheets(early, parts, settings, halves, half_turn, half_block):
    count = sum(part.shape[0] for part in early)
    place = np.arange(2 * halves)
    starts = place % halves * 2 * half_block + place // halves * half_block
    operands = vmem(*parts, basis_pack(0, count, half_turn)) + smem(settings)
    operands += vmem(*early) + table_operands("ramp_drop")
    return call(
        functools.partial(middle_kernel, halves, half_turn, starts, len(early)), "middle_sheets", operands,
        (
            jax.ShapeDtypeStruct((count, HALF_SIDE, SIDE), F32),
            jax.ShapeDtypeStruct((3 * 8 * MODES, HALF_SIDE // 8 * SIDE), BF16),
        ),
        (VMEM_SPEC, VMEM_SPEC),
        [
            pltpu.VMEM((2, 2, KMAX, QUARTER, SIDE), F32),
            shifted_scratch(MODES),
            sheet_scratch(MODES),
        ],
    )


def late_sheets(
    raw, partners, level, dark, modes, settings, groups, offset, halves, half_turn, finished, writes,
):
    count = sum(groups)
    operands = vmem(raw, level, dark, modes, basis_pack(offset, count, half_turn))
    operands += smem(settings) + vmem(*partners) + table_operands("ramp")
    operands += vmem(*finished) if writes == "all" else [(ANY_SPEC, value) for value in finished]
    total = raw.shape[0] // 2 if writes else count
    return call(
        functools.partial(
            late_kernel, halves, offset, groups, writes, len(finished), len(partners)
        ),
        "late_sheets", operands, jax.ShapeDtypeStruct((total, HALF_SIDE, SIDE), F32),
        ANY_SPEC if writes else VMEM_SPEC,
        [
            shifted_scratch(sum(groups)),
            sheet_scratch(count),
            pltpu.SemaphoreType.DMA((len(finished) + len(groups),)),
        ],
        aliases={len(operands) - 1: 0} if writes == "own" else {},
    )


def local(intensity, flat_field, dark_field, correlation, blend_width, padding, cutoff):
    angle_count = lax.axis_size("angle")
    halves = angle_count // 2
    top_bit = angle_count.bit_length() - 2
    angles, local_rows, pixels = intensity.shape
    half_block = angles // 2
    half_turn = half_block * angle_count
    counts = [sum(groups) for groups in CHUNKS]
    starts = [sum(counts[:i]) for i in range(len(counts))]
    raw = intensity.reshape(angles, QUARTER, SIDE)
    partners = [swapped(first_piece(raw, counts[0], halves), "angle", top_bit)]
    mine, other, level, dark = head(
        raw, flat_field.reshape(QUARTER, SIDE), dark_field.reshape(QUARTER, SIDE), halves, half_turn
    )
    settings = jnp.concatenate([correlation, blend_width, padding, cutoff])
    for bit in range(1, top_bit):
        mine = mine + swapped(mine, "angle", bit)
        other = other + swapped(other, "angle", bit)
    received = swapped(other, "angle", 0)
    other_more = swapped(mine, "angle", 0)
    mine_sum, piece = add_modes(raw, mine, received, counts[1:2], starts[1], halves)
    partners.append(swapped(piece, "angle", top_bit))
    far_mine = swapped(mine_sum, "angle", top_bit)
    first, *pieces = early_sheets(
        raw, partners[0], level, dark, (mine_sum, other_more), settings, CHUNKS[0], 0,
        counts[2:4], starts[2], halves,
    )
    partners += [swapped(piece, "angle", top_bit) for piece in pieces]
    far_other = swapped(far_mine, "angle", 0)
    second, *pieces = early_sheets(
        raw, partners[1], level, dark, (far_mine, first), settings, CHUNKS[1], starts[1],
        counts[4:], starts[4] if len(starts) > 4 else 0, halves,
    )
    partners += [swapped(piece, "angle", top_bit) for piece in pieces]
    early = [first, second]
    parts = (mine_sum, other, other_more, far_mine, far_other)
    fixed, modes = middle_sheets(early, parts, settings, halves, half_turn, half_block)
    groups = CHUNKS[2] + CHUNKS[3]
    out = late_sheets(
        raw, partners[2:4], level, dark, modes, settings, groups, starts[2],
        halves, half_turn, [fixed], "all",
    )
    out = late_sheets(
        raw, partners[4:], level, dark, modes, settings, CHUNKS[4], starts[4],
        halves, half_turn, [out], "own",
    )
    return out.reshape(half_block, local_rows, 2 * pixels)


def solution(mesh):
    placed = (P("angle", "row", None), P("row", None), P("row", None), P(), P(), P(), P())
    return jax.shard_map(
        local, mesh=mesh, in_specs=placed, out_specs=P("angle", "row", None), check_vma=False
    )
```

```python
import functools
import math

import jax
import jax.numpy as jnp
import ml_dtypes
import numpy as np
from jax import lax
from jax.experimental import pallas as pl
from jax.experimental.pallas import tpu as pltpu
from jax.sharding import PartitionSpec as P

KMAX = 8
FCUT = 512
SIDE = 128
HALF_SIDE = SIDE // 2
QUARTER = SIDE // 4
MODES = 2 * KMAX
MODE_GROUP = 8
CHUNKS = ((8,8,10),(6,4),(6,6),(4,4),(4,4))
BF16 = jnp.bfloat16
F32 = jnp.float32


def swapped(value, axis, bit):
    mask = 2**bit
    pairs = [(source, source ^ mask) for source in range(lax.axis_size(axis))]
    return lax.ppermute(value, axis, pairs)


def np_split(table):
    high = table.astype(ml_dtypes.bfloat16)
    low = (table - high.astype(np.float64)).astype(ml_dtypes.bfloat16)
    return high, low


@functools.cache
def transform_tables():
    n = SIDE * SIDE
    a = np.arange(SIDE)
    k = np.arange(HALF_SIDE)
    angle = 2 * np.pi * (k[:, None] * a[None, :] % SIDE) / SIDE
    first = np.concatenate([np.cos(angle), -np.sin(angle)])
    first[HALF_SIDE] = 1.0 - 2.0 * (a % 2)
    first_hi, first_lo = np_split(first)
    head = slice(0, HALF_SIDE)
    tail = slice(HALF_SIDE, SIDE)
    first_pack = np.concatenate([first_hi[:, head], first_hi[:, head], first_lo[:, head]], axis=1)
    edge_pack = np.concatenate([first_hi[:, tail], first_lo[:, tail]], axis=1)
    bins = np.stack([k, np.where(k == 0, HALF_SIDE, k)]).reshape(-1)
    turn = 2 * np.pi * (bins[:, None] * a[None, :]) / n
    twiddle = np.concatenate([np.cos(turn), np.sin(turn)], axis=1).astype(np.float32)
    inner = 2 * np.pi * (a[:, None] * a[None, :] % SIDE) / SIDE
    c, s = np.cos(inner), np.sin(inner)
    forward_hi, forward_lo = np_split(np.block([[c, -s], [s, c]]))
    back_hi, back_lo = np_split(np.block([[c, s], [-s, c]]))
    forward = np.concatenate([forward_hi, forward_hi, forward_lo])
    back = np.concatenate([back_hi, back_hi, back_lo])
    f = bins[:, None] + SIDE * a[None, :]
    f = np.minimum(f, n - f).astype(np.float64)
    kept = n // 2
    ramp = f / kept * (1.0 + np.cos(np.pi * f / kept)) / n
    drop = 1.0 - 1.0 / (1.0 + (f / FCUT) ** 8)
    last = 2.0 * first[:, :HALF_SIDE].T
    last[:, 0] = 1.0
    last[:, HALF_SIDE] = 1.0 - 2.0 * (np.arange(HALF_SIDE) % 2)
    last_hi, last_lo = np_split(last)
    last_pack = np.concatenate([last_hi, last_hi, last_lo], axis=1)
    return {
        "first": first_pack,
        "edge": edge_pack,
        "twiddle": twiddle,
        "forward": forward,
        "back": back,
        "ramp": np.concatenate([ramp, ramp], axis=1).astype(np.float32),
        "ramp_drop": np.concatenate([ramp * drop, ramp * drop], axis=1).astype(np.float32),
        "last": last_pack,
    }


@functools.cache
def mode_basis(count, half_turn):
    order = np.arange(KMAX)
    angle = 2 * np.pi * (np.arange(count)[:, None] * order[None, :] % half_turn) / half_turn
    return np.concatenate([np.cos(angle), np.sin(angle)], axis=1)


def phase_rows(starts, half_turn):
    order = np.arange(KMAX)
    angle = 2 * np.pi * (np.asarray(starts)[:, None] * order[None, :] % half_turn) / half_turn
    return np.concatenate([np.cos(angle), np.sin(angle)], axis=1).astype(np.float32)


def split(value):
    high = value.astype(BF16)
    low = (value - high.astype(F32)).astype(BF16)
    return high, low


def dot(left, right):
    return jnp.dot(left, right, preferred_element_type=F32)


def lanes_flipped(block):
    rows = block.shape[0]
    lane = SIDE - 1 - lax.broadcasted_iota(jnp.int32, (rows, SIDE), 1)
    turned = jnp.take_along_axis(block, lane, axis=1)
    row = rows - 1 - lax.broadcasted_iota(jnp.int32, (rows, SIDE), 0)
    return jnp.take_along_axis(turned, row, axis=0)


def flipped(sheet):
    blocks = [lanes_flipped(sheet[8 * i : 8 * i + 8]) for i in range(QUARTER // 8)]
    return jnp.concatenate(blocks[::-1], axis=0)


def swap_first_rows(upper_part, lower_part):
    row = lax.broadcasted_iota(jnp.int32, upper_part.shape, 0)
    return (
        jnp.where(row == 0, lower_part, upper_part),
        jnp.where(row == 0, upper_part, lower_part),
    )


def blend_weight(correlation, blend):
    position = (
        lax.broadcasted_iota(jnp.int32, (HALF_SIDE, SIDE), 0) * SIDE
        + lax.broadcasted_iota(jnp.int32, (HALF_SIDE, SIDE), 1)
    ).astype(F32)
    pixels = QUARTER * SIDE
    center = pixels - correlation.astype(F32) / 2.0
    return jnp.clip((position + 0.5 - center) / blend.astype(F32) + 0.5, 0.0, 1.0)


def edge_response(edge_table, padding):
    index = (
        lax.broadcasted_iota(jnp.int32, (HALF_SIDE, SIDE), 0) * SIDE
        + lax.broadcasted_iota(jnp.int32, (HALF_SIDE, SIDE), 1)
    )
    after = (index < padding).astype(F32)
    before = (index >= HALF_SIDE * SIDE - padding).astype(F32)
    boxes = jnp.concatenate([after, before], axis=1)
    boxes = jnp.concatenate([boxes, boxes], axis=0).astype(BF16)
    return dot(edge_table, boxes)


def transform_group(views, weight, correlation, edges, tables, gain, shifted, base, emit):
    count = len(views)
    whole = correlation // SIDE
    part = correlation % SIDE
    lane = lax.broadcasted_iota(jnp.int32, (HALF_SIDE, SIDE), 1)
    in_row = lane < SIDE - part
    keep = 1.0 - weight[:QUARTER]
    stitched = []
    for i, view in enumerate(views):
        main, back = view()
        rolled = pltpu.roll(main, SIDE - part, 1)
        last = jnp.broadcast_to(main[QUARTER - 1 :, SIDE - 1 :], (QUARTER + 8, SIDE))
        shifted[base + i, QUARTER : 2 * QUARTER, :] = rolled
        shifted[base + i, 2 * QUARTER :, :] = last
        right = jnp.where(
            in_row,
            shifted[base + i, pl.ds(whole, HALF_SIDE), :],
            shifted[base + i, pl.ds(whole + 1, HALF_SIDE), :],
        )
        sheet = weight * right
        top = sheet[:QUARTER] + keep * flipped(back)
        stitched.append(jnp.concatenate([top, sheet[QUARTER:]], axis=0))
    high, low = split(jnp.concatenate(stitched, axis=1))
    grown = dot(tables["first"][...], jnp.concatenate([high, low, high], axis=0))
    yield
    after, before = edges[:, :SIDE], edges[:, SIDE:]
    cos_turn, sin_turn = tables["twiddle"][:, :SIDE], tables["twiddle"][:, SIDE:]
    real, imag = [], []
    for i, sheet in enumerate(stitched):
        ends = (
            grown[:, i * SIDE : (i + 1) * SIDE]
            + sheet[HALF_SIDE - 1 :, SIDE - 1 :] * after
            + sheet[:1, :1] * before
        )
        real.append(ends[:HALF_SIDE])
        imag.append(ends[HALF_SIDE:])
    for i in range(0, count, 2):
        imag[i], real[i + 1] = swap_first_rows(imag[i], real[i + 1])
    turned = []
    for i in range(count):
        rows = slice((i % 2) * HALF_SIDE, (i % 2 + 1) * HALF_SIDE)
        c, s = cos_turn[rows], sin_turn[rows]
        turned.append(jnp.concatenate([real[i] * c + imag[i] * s, imag[i] * c - real[i] * s], axis=1))
    high, low = split(jnp.concatenate(turned, axis=0))
    spectrum = dot(jnp.concatenate([high, low, high], axis=1), tables["forward"][...])
    yield
    gains = jnp.concatenate([gain[...]] * (count // 2), axis=0)
    high, low = split(spectrum * gains)
    inner = dot(jnp.concatenate([high, low, high], axis=1), tables["back"][...])
    yield
    real, imag = [], []
    for i in range(count):
        rows = slice((i % 2) * HALF_SIDE, (i % 2 + 1) * HALF_SIDE)
        c, s = cos_turn[rows], sin_turn[rows]
        block = inner[i * HALF_SIDE : (i + 1) * HALF_SIDE]
        real.append(block[:, :SIDE] * c - block[:, SIDE:] * s)
        imag.append(block[:, SIDE:] * c + block[:, :SIDE] * s)
    for i in range(0, count, 2):
        imag[i], real[i + 1] = swap_first_rows(imag[i], real[i + 1])
    columns = jnp.concatenate(
        [jnp.concatenate([real[i], imag[i]], axis=0) for i in range(count)], axis=1
    )
    high, low = split(columns)
    result = dot(tables["last"][...], jnp.concatenate([high, low, high], axis=0))
    yield
    emit(base, [result[:, i * SIDE : (i + 1) * SIDE] for i in range(count)])


def take_turns(groups):
    groups = list(groups)
    while groups:
        for group in list(groups):
            if next(group, groups) is groups:
                groups.remove(group)


TABLES = ("first", "edge", "twiddle", "forward", "back", "last")


def picked(place, values):
    result = jnp.float32(values[-1])
    for i, value in enumerate(values[:-1]):
        result = jnp.where(place == i, jnp.float32(value), result)
    return result


def rotations(place, starts, half_turn):
    table = phase_rows(starts, half_turn)
    cos = [picked(place, list(table[:, k])) for k in range(KMAX)]
    sin = [picked(place, list(table[:, KMAX + k])) for k in range(KMAX)]
    return cos, sin


def send_from(raw, halves):
    return jnp.where(lax.axis_index("angle") >= halves, 0, raw.shape[0] // 2)


def start_pieces(halves, offset, raw, pieces, sems):
    start = send_from(raw, halves) + offset
    copies = []
    for i, piece in enumerate(pieces):
        count = piece.shape[0]
        copies.append(pltpu.make_async_copy(raw.at[pl.ds(start, count)], piece, sems.at[i]))
        copies[-1].start()
        start = start + count
    return copies


def head_kernel(
    halves, half_turn, raw_far, flat_far, dark_far, basis_far,
    mine, other, level, dark, raw, flat, basis, sems,
):
    blocks = 4
    block = raw.shape[0] // blocks
    pairs = [(flat_far, flat), (dark_far, dark), (basis_far, basis)]
    for i in range(blocks):
        rows = pl.ds(i * block, block)
        pairs.append((raw_far.at[rows], raw.at[rows]))
    copies = [
        pltpu.make_async_copy(source, target, sems.at[i])
        for i, (source, target) in enumerate(pairs)
    ]
    for copy in copies:
        copy.start()
    copies[0].wait()
    copies[1].wait()
    level[...] = jnp.log(flat[...] - dark[...])
    turns = phase_rows(np.arange(blocks) * block, half_turn)
    cos_total, sin_total = [0.0] * KMAX, [0.0] * KMAX
    for i in range(blocks):
        copies[3 + i].wait()
        projected = level[...] - jnp.log(raw[i * block : (i + 1) * block] - dark[...])
        columns = jnp.concatenate(
            [
                projected[:, 8 * j : 8 * j + 8, :].reshape(block * 8, SIDE)
                for j in range(QUARTER // 8)
            ],
            axis=1,
        )
        high, low = split(columns)
        if i == 0:
            copies[2].wait()
        partial = dot(basis[...], jnp.concatenate([high, low, high], axis=0))
        for k in range(KMAX):
            c, s = float(turns[i, k]), float(turns[i, KMAX + k])
            cos_part = partial[8 * k : 8 * k + 8, :]
            sin_part = partial[8 * (KMAX + k) : 8 * (KMAX + k) + 8, :]
            cos_total[k] = cos_total[k] + (cos_part * c - sin_part * s)
            sin_total[k] = sin_total[k] + (sin_part * c + cos_part * s)
    place = lax.axis_index("angle")
    cos, sin = rotations(place % halves, np.arange(halves) * raw.shape[0], half_turn)
    odd = place % 2
    half = KMAX // 2
    for k in range(KMAX):
        cos_mode = cos_total[k] * cos[k] - sin_total[k] * sin[k]
        sin_mode = sin_total[k] * cos[k] + cos_total[k] * sin[k]
        spot = k % half
        is_mine = odd == k // half

        def put(ref):
            for i in range(QUARTER // 8):
                lanes = slice(i * SIDE, (i + 1) * SIDE)
                ref[spot, 8 * i : 8 * i + 8, :] = cos_mode[:, lanes]
                ref[half + spot, 8 * i : 8 * i + 8, :] = sin_mode[:, lanes]

        @pl.when(is_mine)
        def _():
            put(mine)

        @pl.when(jnp.logical_not(is_mine))
        def _():
            put(other)


def piece_kernel(halves, raw_far, piece, sems):
    start_pieces(halves, 0, raw_far, [piece], sems)[0].wait()


def add_kernel(halves, offset, raw, mine, received, *refs):
    total, *refs = refs[4:]
    pieces, sems = refs[:-1], refs[-1]
    copies = start_pieces(halves, offset, raw, pieces, sems)
    total[...] = mine[...] + received[...]
    for copy in copies:
        copy.wait()


def filter_modes(
    halves, half_turn, mine, other_a, other_b, far_mine, far_other,
    weight, correlation, edges, cutoff, starts, tables, modes, side, shifted, result,
):
    place = lax.axis_index("angle")
    odd = place % 2
    upper = place // halves
    half = KMAX // 2
    side[upper, odd] = mine[...]
    side[upper, 1 - odd] = other_a[...] + other_b[...]
    side[1 - upper, odd] = far_mine[...]
    side[1 - upper, 1 - odd] = far_other[...]

    def view(m):
        return lambda: (side[0, m // KMAX, m % KMAX], side[1, m // KMAX, m % KMAX])

    def emit(first, sheets):
        for i, sheet in enumerate(sheets):
            result[first + i] = sheet

    take_turns(
        transform_group(
            [view(m) for m in range(first, first + MODE_GROUP)],
            weight, correlation, edges, tables, tables["ramp_drop"], shifted, first, emit,
        )
        for first in range(0, MODES, MODE_GROUP)
    )
    cos, sin = rotations(place, starts, half_turn)
    for k in range(KMAX):
        spot = (k // half) * KMAX + k % half
        scale = jnp.where(k < cutoff, (1.0 if k == 0 else 2.0) / half_turn, 0.0)
        c = cos[k] * scale
        s = sin[k] * scale
        cos_sheet, sin_sheet = result[spot], result[spot + half]
        for row, sheet in (
            (k, cos_sheet * c + sin_sheet * s),
            (KMAX + k, sin_sheet * c - cos_sheet * s),
        ):
            high, low = split(sheet)
            for i in range(HALF_SIDE // 8):
                lanes = slice(i * SIDE, (i + 1) * SIDE)
                for part, value in enumerate((high, low, high)):
                    place_row = part * 8 * MODES + 8 * row
                    modes[place_row : place_row + 8, lanes] = value[8 * i : 8 * i + 8]


def low_sheets(basis, modes):
    low = dot(basis, modes)

    def block(i, j):
        return low[8 * i : 8 * i + 8, j * SIDE : (j + 1) * SIDE]

    return block


def clean_rows(
    halves, offset, groups, raw, partner, level, dark, weight, correlation, edges, tables, shifted, emit,
    beside=(),
):
    is_upper = lax.axis_index("angle") >= halves
    start = jnp.where(is_upper, raw.shape[0] // 2, 0) + offset

    def view(i):
        def load():
            here = level[...] - jnp.log(raw[start + i] - dark[...])
            there = level[...] - jnp.log(partner[i] - dark[...])
            return jnp.where(is_upper, there, here), jnp.where(is_upper, here, there)

        return load

    firsts = [sum(groups[:i]) for i in range(len(groups))]
    turns = [
        transform_group(
            [view(i) for i in range(first, first + size)],
            weight, correlation, edges, tables, tables["ramp"], shifted, first, emit,
        )
        for first, size in zip(firsts, groups)
    ]
    take_turns(turns + list(beside))


def prepare(settings, tables, shifted):
    shifted[:, :QUARTER, :] = jnp.zeros((shifted.shape[0], QUARTER, SIDE), F32)
    weight = blend_weight(settings[0], settings[1])
    return weight, edge_response(tables["edge"][...], settings[2])


def early_kernel(
    halves, offset, next_offset, groups, waits, raw, partner, level, dark, *refs,
):
    settings, refs = [ref[0] for ref in refs[:4]], refs[4:]
    refs = refs[waits:]
    names = TABLES + ("ramp",)
    tables = dict(zip(names, refs))
    out, *pieces, shifted, sems = refs[len(names) :]
    copies = start_pieces(halves, next_offset, raw, pieces, sems)
    weight, edges = prepare(settings, tables, shifted)

    def emit(first, sheets):
        for i, sheet in enumerate(sheets):
            out[first + i] = sheet

    clean_rows(
        halves, offset, groups, raw, partner, level, dark, weight, settings[0], edges, tables, shifted, emit
    )
    for copy in copies:
        copy.wait()


def middle_kernel(
    halves, half_turn, starts, early_count, mine, other_a, other_b, far_mine, far_other, basis,
    *refs,
):
    settings, refs = [ref[0] for ref in refs[:4]], refs[4:]
    names = TABLES + ("ramp_drop",)
    early, refs = refs[:early_count], refs[early_count:]
    tables = dict(zip(names, refs))
    fixed, modes, side, shifted, result = refs[len(names) :]
    weight, edges = prepare(settings, tables, shifted)
    filter_modes(
        halves, half_turn, mine, other_a, other_b, far_mine, far_other,
        weight, settings[0], edges, settings[3], starts, tables, modes, side, shifted, result,
    )
    low = low_sheets(basis[...], modes[...])
    row = 0
    for part in early:
        for i in range(part.shape[0]):
            for j in range(HALF_SIDE // 8):
                fixed[row, 8 * j : 8 * j + 8, :] = part[i, 8 * j : 8 * j + 8, :] - low(row, j)
            row += 1


class Joined:
    def __init__(self, refs):
        self.rows = [(ref, i) for ref in refs for i in range(ref.shape[0])]

    def __getitem__(self, row):
        ref, i = self.rows[row]
        return ref[i]


def late_kernel(
    halves, offset, groups, partner_count, writes, raw, level, dark, modes, basis, finished, *refs,
):
    settings, refs = [ref[0] for ref in refs[:4]], refs[4:]
    names = TABLES + ("ramp",)
    partner, refs = Joined(refs[:partner_count]), refs[partner_count:]
    tables = dict(zip(names, refs))
    refs = refs[len(names) :]
    out, done, shifted, sems = refs[1:] if writes else refs
    copies = []

    def send(source, first):
        target = out.at[pl.ds(first, source.shape[0])]
        copies.append(pltpu.make_async_copy(source, target, sems.at[len(copies)]))
        copies[-1].start()

    send(finished, offset - finished.shape[0])
    weight, edges = prepare(settings, tables, shifted)
    lows = []

    def low_turn():
        lows.append(low_sheets(basis[...], modes[...]))
        yield

    def emit(first, sheets):
        for i, sheet in enumerate(sheets):
            for j in range(HALF_SIDE // 8):
                done[first + i, 8 * j : 8 * j + 8, :] = (
                    sheet[8 * j : 8 * j + 8] - lows[0](first + i, j)
                )
        if writes:
            send(done.at[pl.ds(first, len(sheets))], offset + first)

    clean_rows(
        halves, offset, groups, raw, partner, level, dark, weight, settings[0], edges, tables, shifted, emit,
        [low_turn()],
    )
    for copy in copies:
        copy.wait()


VMEM_SPEC = pl.BlockSpec(memory_space=pltpu.VMEM)
SMEM_SPEC = pl.BlockSpec(memory_space=pltpu.SMEM)
ANY_SPEC = pl.BlockSpec(memory_space=pl.ANY)
MIB = 2**20
HEAD_COST = 16 * MIB


def call(kernel, name, operands, out_shape, out_specs, scratch, limit=32 * MIB, aliases=(), cost=0):
    specs = [spec for spec, _ in operands]
    return pl.pallas_call(
        kernel,
        out_shape=out_shape,
        in_specs=specs,
        out_specs=out_specs,
        scratch_shapes=scratch,
        input_output_aliases=dict(aliases),
        compiler_params=pltpu.CompilerParams(vmem_limit_bytes=limit),
        cost_estimate=pl.CostEstimate(flops=0, bytes_accessed=cost, transcendentals=0),
        name=name,
    )(*(value for _, value in operands))


def vmem(*values):
    return [(VMEM_SPEC, jnp.asarray(value)) for value in values]


def smem(*values):
    return [(SMEM_SPEC, jnp.asarray(value)) for value in values]


def table_operands(*extra):
    tables = transform_tables()
    return vmem(*(tables[name] for name in TABLES + extra))


def shifted_scratch(count):
    return pltpu.VMEM((count, 3 * QUARTER + 8, SIDE), F32)


def sheet_scratch(count):
    return pltpu.VMEM((count, HALF_SIDE, SIDE), F32)


def basis_pack(offset, count, half_turn):
    basis = np.kron(mode_basis(offset + count, half_turn)[offset:], np.eye(8))
    hi, lo = np_split(basis)
    return np.concatenate([hi, hi, lo], axis=1)


def far(*values):
    return [
        (ANY_SPEC, pltpu.with_memory_space_constraint(jnp.asarray(value), pltpu.HBM))
        for value in values
    ]


def piece_shapes(raw, counts):
    return [jax.ShapeDtypeStruct((count,) + raw.shape[1:], F32) for count in counts]


def head(raw, flat, dark, halves, half_turn):
    block = raw.shape[0] // 4
    hi, lo = np_split(np.kron(mode_basis(block, half_turn).T, np.eye(8)))
    basis = np.concatenate([hi, hi, lo], axis=1)
    shapes = [jax.ShapeDtypeStruct((KMAX, QUARTER, SIDE), F32)] * 2
    shapes += [jax.ShapeDtypeStruct((QUARTER, SIDE), F32)] * 2
    return call(
        functools.partial(head_kernel, halves, half_turn), "head",
        far(raw, flat, dark, basis), shapes, [VMEM_SPEC] * len(shapes),
        [
            pltpu.VMEM(raw.shape, F32),
            pltpu.VMEM(flat.shape, F32),
            pltpu.VMEM(basis.shape, BF16),
            pltpu.SemaphoreType.DMA((7,)),
        ],
        cost=HEAD_COST,
    )


def first_piece(raw, count, halves):
    return call(
        functools.partial(piece_kernel, halves), "first_piece", far(raw),
        piece_shapes(raw, [count])[0], VMEM_SPEC, [pltpu.SemaphoreType.DMA((1,))],
    )


def add_modes(raw, mine, received, settings, counts, offset, halves):
    shapes = [jax.ShapeDtypeStruct(mine.shape, F32)] + piece_shapes(raw, counts)
    return call(
        functools.partial(add_kernel, halves, offset), "add_modes",
        vmem(raw, mine, received) + smem(*settings),
        shapes, [VMEM_SPEC] * len(shapes), [pltpu.SemaphoreType.DMA((len(counts),))],
    )


def early_sheets(raw, partner, level, dark, after, settings, groups, offset, counts, next_offset, halves):
    operands = vmem(raw, partner, level, dark) + smem(*settings)
    operands += [(ANY_SPEC, value) for value in after] + table_operands("ramp")
    shapes = [jax.ShapeDtypeStruct((sum(groups), HALF_SIDE, SIDE), F32)] + piece_shapes(raw, counts)
    return call(
        functools.partial(early_kernel, halves, offset, next_offset, groups, len(after)), "early_sheets",
        operands, shapes, [VMEM_SPEC] * len(shapes),
        [shifted_scratch(sum(groups)), pltpu.SemaphoreType.DMA((max(len(counts), 1),))],
    )


def middle_sheets(early, parts, settings, halves, half_turn, half_block):
    count = sum(part.shape[0] for part in early)
    place = np.arange(2 * halves)
    starts = place % halves * 2 * half_block + place // halves * half_block
    operands = vmem(*parts, basis_pack(0, count, half_turn)) + smem(*settings)
    operands += vmem(*early) + table_operands("ramp_drop")
    return call(
        functools.partial(middle_kernel, halves, half_turn, starts, len(early)), "middle_sheets", operands,
        (
            jax.ShapeDtypeStruct((count, HALF_SIDE, SIDE), F32),
            jax.ShapeDtypeStruct((3 * 8 * MODES, HALF_SIDE // 8 * SIDE), BF16),
        ),
        (VMEM_SPEC, VMEM_SPEC),
        [
            pltpu.VMEM((2, 2, KMAX, QUARTER, SIDE), F32),
            shifted_scratch(MODES),
            sheet_scratch(MODES),
        ],
    )


def late_sheets(
    raw, partners, level, dark, modes, settings, groups, offset, halves, half_turn, finished, out=None,
):
    count = sum(groups)
    writes = out is not None
    operands = vmem(raw, level, dark, modes, basis_pack(offset, count, half_turn), finished)
    operands += smem(*settings) + vmem(*partners) + table_operands("ramp")
    aliases = {}
    if writes:
        aliases = {len(operands): 0}
        operands.append((ANY_SPEC, out))
    result = jax.ShapeDtypeStruct((raw.shape[0] // 2, HALF_SIDE, SIDE), F32)
    rows = jax.ShapeDtypeStruct((count, HALF_SIDE, SIDE), F32)
    scratch = [shifted_scratch(count), pltpu.SemaphoreType.DMA((1 + len(groups),))]
    return call(
        functools.partial(late_kernel, halves, offset, groups, len(partners), writes), "late_sheets",
        operands, [result] if writes else [result, rows],
        [ANY_SPEC] if writes else [ANY_SPEC, VMEM_SPEC],
        [sheet_scratch(count)] * writes + scratch, aliases=aliases,
    )


def local(intensity, flat_field, dark_field, correlation, blend_width, padding, cutoff):
    angle_count = lax.axis_size("angle")
    halves = angle_count // 2
    top_bit = angle_count.bit_length() - 2
    angles, local_rows, pixels = intensity.shape
    half_block = angles // 2
    half_turn = half_block * angle_count
    counts = [sum(groups) for groups in CHUNKS]
    starts = [sum(counts[:i]) for i in range(len(counts))]
    raw = intensity.reshape(angles, QUARTER, SIDE)
    partners = [swapped(first_piece(raw, counts[0], halves), "angle", top_bit)]
    mine, other, level, dark = head(
        raw, flat_field.reshape(QUARTER, SIDE), dark_field.reshape(QUARTER, SIDE), halves, half_turn
    )
    settings = (correlation, blend_width, padding, cutoff)
    for bit in range(1, top_bit):
        mine = mine + swapped(mine, "angle", bit)
        other = other + swapped(other, "angle", bit)
    received = swapped(other, "angle", 0)
    other_more = swapped(mine, "angle", 0)
    mine_sum, piece = add_modes(raw, mine, received, settings, counts[1:2], starts[1], halves)
    partners.append(swapped(piece, "angle", top_bit))
    far_mine = swapped(mine_sum, "angle", top_bit)
    first, *pieces = early_sheets(
        raw, partners[0], level, dark, (mine_sum, other_more), settings, CHUNKS[0], 0,
        counts[2:4], starts[2], halves,
    )
    partners += [swapped(piece, "angle", top_bit) for piece in pieces]
    far_other = swapped(far_mine, "angle", 0)
    second, *pieces = early_sheets(
        raw, partners[1], level, dark, (far_mine, first), settings, CHUNKS[1], starts[1],
        counts[4:], starts[4] if len(starts) > 4 else 0, halves,
    )
    partners += [swapped(piece, "angle", top_bit) for piece in pieces]
    early = [first, second]
    parts = (mine_sum, other, other_more, far_mine, far_other)
    fixed, modes = middle_sheets(early, parts, settings, halves, half_turn, half_block)
    out, late = late_sheets(
        raw, partners[2:4], level, dark, modes, settings, CHUNKS[2] + CHUNKS[3], starts[2],
        halves, half_turn, fixed,
    )
    (out,) = late_sheets(
        raw, partners[4:], level, dark, modes, settings, CHUNKS[4], starts[4],
        halves, half_turn, late, out,
    )
    return out.reshape(half_block, local_rows, 2 * pixels)


def solution(mesh):
    placed = (P("angle", "row", None), P("row", None), P("row", None), P(), P(), P(), P())
    return jax.shard_map(
        local, mesh=mesh, in_specs=placed, out_specs=P("angle", "row", None), check_vma=False
    )
```

```python
import functools
import math

import jax
import jax.numpy as jnp
import ml_dtypes
import numpy as np
from jax import lax
from jax.experimental import pallas as pl
from jax.experimental.pallas import tpu as pltpu
from jax.sharding import PartitionSpec as P

KMAX = 8
FCUT = 512
SIDE = 128
HALF_SIDE = SIDE // 2
QUARTER = SIDE // 4
MODES = 2 * KMAX
MODE_GROUP = 8
CHUNKS = ((12, 16), (4, 4, 4), (4, 4, 4, 2), (2, 4), (4,))
BF16 = jnp.bfloat16
F32 = jnp.float32


def swapped(value, axis, bit):
    mask = 2**bit
    pairs = [(source, source ^ mask) for source in range(lax.axis_size(axis))]
    return lax.ppermute(value, axis, pairs)


def np_split(table):
    high = table.astype(ml_dtypes.bfloat16)
    low = (table - high.astype(np.float64)).astype(ml_dtypes.bfloat16)
    return high, low


@functools.cache
def transform_tables():
    n = SIDE * SIDE
    a = np.arange(SIDE)
    k = np.arange(HALF_SIDE)
    angle = 2 * np.pi * (k[:, None] * a[None, :] % SIDE) / SIDE
    first = np.concatenate([np.cos(angle), -np.sin(angle)])
    first[HALF_SIDE] = 1.0 - 2.0 * (a % 2)
    first_hi, first_lo = np_split(first)
    head = slice(0, HALF_SIDE)
    tail = slice(HALF_SIDE, SIDE)
    first_pack = np.concatenate([first_hi[:, head], first_hi[:, head], first_lo[:, head]], axis=1)
    edge_pack = np.concatenate([first_hi[:, tail], first_lo[:, tail]], axis=1)
    bins = np.stack([k, np.where(k == 0, HALF_SIDE, k)]).reshape(-1)
    turn = 2 * np.pi * (bins[:, None] * a[None, :]) / n
    twiddle = np.concatenate([np.cos(turn), np.sin(turn)], axis=1).astype(np.float32)
    inner = 2 * np.pi * (a[:, None] * a[None, :] % SIDE) / SIDE
    c, s = np.cos(inner), np.sin(inner)
    forward_hi, forward_lo = np_split(np.block([[c, -s], [s, c]]))
    back_hi, back_lo = np_split(np.block([[c, s], [-s, c]]))
    forward = np.concatenate([forward_hi, forward_hi, forward_lo])
    back = np.concatenate([back_hi, back_hi, back_lo])
    f = bins[:, None] + SIDE * a[None, :]
    f = np.minimum(f, n - f).astype(np.float64)
    kept = n // 2
    ramp = f / kept * (1.0 + np.cos(np.pi * f / kept)) / n
    drop = 1.0 - 1.0 / (1.0 + (f / FCUT) ** 8)
    last = 2.0 * first[:, :HALF_SIDE].T
    last[:, 0] = 1.0
    last[:, HALF_SIDE] = 1.0 - 2.0 * (np.arange(HALF_SIDE) % 2)
    last_hi, last_lo = np_split(last)
    last_pack = np.concatenate([last_hi, last_hi, last_lo], axis=1)
    return {
        "first": first_pack,
        "edge": edge_pack,
        "twiddle": twiddle,
        "forward": forward,
        "back": back,
        "ramp": np.concatenate([ramp, ramp], axis=1).astype(np.float32),
        "ramp_drop": np.concatenate([ramp * drop, ramp * drop], axis=1).astype(np.float32),
        "last": last_pack,
    }


@functools.cache
def mode_basis(count, half_turn):
    order = np.arange(KMAX)
    angle = 2 * np.pi * (np.arange(count)[:, None] * order[None, :] % half_turn) / half_turn
    return np.concatenate([np.cos(angle), np.sin(angle)], axis=1)


def phase_rows(starts, half_turn):
    order = np.arange(KMAX)
    angle = 2 * np.pi * (np.asarray(starts)[:, None] * order[None, :] % half_turn) / half_turn
    return np.concatenate([np.cos(angle), np.sin(angle)], axis=1).astype(np.float32)


def split(value):
    high = value.astype(BF16)
    low = (value - high.astype(F32)).astype(BF16)
    return high, low


def dot(left, right):
    return jnp.dot(left, right, preferred_element_type=F32)


def lanes_flipped(block):
    rows = block.shape[0]
    lane = SIDE - 1 - lax.broadcasted_iota(jnp.int32, (rows, SIDE), 1)
    turned = jnp.take_along_axis(block, lane, axis=1)
    row = rows - 1 - lax.broadcasted_iota(jnp.int32, (rows, SIDE), 0)
    return jnp.take_along_axis(turned, row, axis=0)


def flipped(sheet):
    blocks = [lanes_flipped(sheet[8 * i : 8 * i + 8]) for i in range(QUARTER // 8)]
    return jnp.concatenate(blocks[::-1], axis=0)


def swap_first_rows(upper_part, lower_part):
    row = lax.broadcasted_iota(jnp.int32, upper_part.shape, 0)
    return (
        jnp.where(row == 0, lower_part, upper_part),
        jnp.where(row == 0, upper_part, lower_part),
    )


def blend_weight(correlation, blend):
    position = (
        lax.broadcasted_iota(jnp.int32, (HALF_SIDE, SIDE), 0) * SIDE
        + lax.broadcasted_iota(jnp.int32, (HALF_SIDE, SIDE), 1)
    ).astype(F32)
    pixels = QUARTER * SIDE
    center = pixels - correlation.astype(F32) / 2.0
    return jnp.clip((position + 0.5 - center) / blend.astype(F32) + 0.5, 0.0, 1.0)


def edge_response(edge_table, padding):
    index = (
        lax.broadcasted_iota(jnp.int32, (HALF_SIDE, SIDE), 0) * SIDE
        + lax.broadcasted_iota(jnp.int32, (HALF_SIDE, SIDE), 1)
    )
    after = (index < padding).astype(F32)
    before = (index >= HALF_SIDE * SIDE - padding).astype(F32)
    boxes = jnp.concatenate([after, before], axis=1)
    boxes = jnp.concatenate([boxes, boxes], axis=0).astype(BF16)
    return dot(edge_table, boxes)


def transform_group(views, weight, correlation, edges, tables, gain, shifted, base, emit):
    count = len(views)
    whole = correlation // SIDE
    part = correlation % SIDE
    lane = lax.broadcasted_iota(jnp.int32, (HALF_SIDE, SIDE), 1)
    in_row = lane < SIDE - part
    keep = 1.0 - weight[:QUARTER]
    stitched = []
    for i, view in enumerate(views):
        main, back = view()
        rolled = pltpu.roll(main, SIDE - part, 1)
        last = jnp.broadcast_to(main[QUARTER - 1 :, SIDE - 1 :], (QUARTER + 8, SIDE))
        shifted[base + i, QUARTER : 2 * QUARTER, :] = rolled
        shifted[base + i, 2 * QUARTER :, :] = last
        right = jnp.where(
            in_row,
            shifted[base + i, pl.ds(whole, HALF_SIDE), :],
            shifted[base + i, pl.ds(whole + 1, HALF_SIDE), :],
        )
        sheet = weight * right
        top = sheet[:QUARTER] + keep * flipped(back)
        stitched.append(jnp.concatenate([top, sheet[QUARTER:]], axis=0))
    high, low = split(jnp.concatenate(stitched, axis=1))
    grown = dot(tables["first"][...], jnp.concatenate([high, low, high], axis=0))
    yield
    after, before = edges[:, :SIDE], edges[:, SIDE:]
    cos_turn, sin_turn = tables["twiddle"][:, :SIDE], tables["twiddle"][:, SIDE:]
    real, imag = [], []
    for i, sheet in enumerate(stitched):
        ends = (
            grown[:, i * SIDE : (i + 1) * SIDE]
            + sheet[HALF_SIDE - 1 :, SIDE - 1 :] * after
            + sheet[:1, :1] * before
        )
        real.append(ends[:HALF_SIDE])
        imag.append(ends[HALF_SIDE:])
    for i in range(0, count, 2):
        imag[i], real[i + 1] = swap_first_rows(imag[i], real[i + 1])
    turned = []
    for i in range(count):
        rows = slice((i % 2) * HALF_SIDE, (i % 2 + 1) * HALF_SIDE)
        c, s = cos_turn[rows], sin_turn[rows]
        turned.append(jnp.concatenate([real[i] * c + imag[i] * s, imag[i] * c - real[i] * s], axis=1))
    high, low = split(jnp.concatenate(turned, axis=0))
    spectrum = dot(jnp.concatenate([high, low, high], axis=1), tables["forward"][...])
    yield
    gains = jnp.concatenate([gain[...]] * (count // 2), axis=0)
    high, low = split(spectrum * gains)
    inner = dot(jnp.concatenate([high, low, high], axis=1), tables["back"][...])
    yield
    real, imag = [], []
    for i in range(count):
        rows = slice((i % 2) * HALF_SIDE, (i % 2 + 1) * HALF_SIDE)
        c, s = cos_turn[rows], sin_turn[rows]
        block = inner[i * HALF_SIDE : (i + 1) * HALF_SIDE]
        real.append(block[:, :SIDE] * c - block[:, SIDE:] * s)
        imag.append(block[:, SIDE:] * c + block[:, :SIDE] * s)
    for i in range(0, count, 2):
        imag[i], real[i + 1] = swap_first_rows(imag[i], real[i + 1])
    columns = jnp.concatenate(
        [jnp.concatenate([real[i], imag[i]], axis=0) for i in range(count)], axis=1
    )
    high, low = split(columns)
    result = dot(tables["last"][...], jnp.concatenate([high, low, high], axis=0))
    yield
    emit(base, [result[:, i * SIDE : (i + 1) * SIDE] for i in range(count)])


def take_turns(groups):
    groups = list(groups)
    while groups:
        for group in list(groups):
            if next(group, groups) is groups:
                groups.remove(group)


TABLES = ("first", "edge", "twiddle", "forward", "back", "last")


def picked(place, values):
    result = jnp.float32(values[-1])
    for i, value in enumerate(values[:-1]):
        result = jnp.where(place == i, jnp.float32(value), result)
    return result


def rotations(place, starts, half_turn):
    table = phase_rows(starts, half_turn)
    cos = [picked(place, list(table[:, k])) for k in range(KMAX)]
    sin = [picked(place, list(table[:, KMAX + k])) for k in range(KMAX)]
    return cos, sin


def send_from(raw, halves):
    return jnp.where(lax.axis_index("angle") >= halves, 0, raw.shape[0] // 2)


def start_pieces(halves, offset, raw, pieces, sems):
    start = send_from(raw, halves) + offset
    copies = []
    for i, piece in enumerate(pieces):
        count = piece.shape[0]
        copies.append(pltpu.make_async_copy(raw.at[pl.ds(start, count)], piece, sems.at[i]))
        copies[-1].start()
        start = start + count
    return copies


def head_kernel(
    halves, half_turn, raw_far, flat_far, dark_far, basis_far,
    mine, other, level, dark, raw, flat, basis, sems,
):
    blocks = 4
    block = raw.shape[0] // blocks
    pairs = [(flat_far, flat), (dark_far, dark), (basis_far, basis)]
    for i in range(blocks):
        rows = pl.ds(i * block, block)
        pairs.append((raw_far.at[rows], raw.at[rows]))
    copies = [
        pltpu.make_async_copy(source, target, sems.at[i])
        for i, (source, target) in enumerate(pairs)
    ]
    for copy in copies:
        copy.start()
    copies[0].wait()
    copies[1].wait()
    level[...] = jnp.log(flat[...] - dark[...])
    turns = phase_rows(np.arange(blocks) * block, half_turn)
    cos_total, sin_total = [0.0] * KMAX, [0.0] * KMAX
    for i in range(blocks):
        copies[3 + i].wait()
        projected = level[...] - jnp.log(raw[i * block : (i + 1) * block] - dark[...])
        columns = jnp.concatenate(
            [
                projected[:, 8 * j : 8 * j + 8, :].reshape(block * 8, SIDE)
                for j in range(QUARTER // 8)
            ],
            axis=1,
        )
        high, low = split(columns)
        if i == 0:
            copies[2].wait()
        partial = dot(basis[...], jnp.concatenate([high, low, high], axis=0))
        for k in range(KMAX):
            c, s = float(turns[i, k]), float(turns[i, KMAX + k])
            cos_part = partial[8 * k : 8 * k + 8, :]
            sin_part = partial[8 * (KMAX + k) : 8 * (KMAX + k) + 8, :]
            cos_total[k] = cos_total[k] + (cos_part * c - sin_part * s)
            sin_total[k] = sin_total[k] + (sin_part * c + cos_part * s)
    place = lax.axis_index("angle")
    cos, sin = rotations(place % halves, np.arange(halves) * raw.shape[0], half_turn)
    odd = place % 2
    half = KMAX // 2
    for k in range(KMAX):
        cos_mode = cos_total[k] * cos[k] - sin_total[k] * sin[k]
        sin_mode = sin_total[k] * cos[k] + cos_total[k] * sin[k]
        spot = k % half
        is_mine = odd == k // half

        def put(ref):
            for i in range(QUARTER // 8):
                lanes = slice(i * SIDE, (i + 1) * SIDE)
                ref[spot, 8 * i : 8 * i + 8, :] = cos_mode[:, lanes]
                ref[half + spot, 8 * i : 8 * i + 8, :] = sin_mode[:, lanes]

        @pl.when(is_mine)
        def _():
            put(mine)

        @pl.when(jnp.logical_not(is_mine))
        def _():
            put(other)


def piece_kernel(halves, raw_far, piece, sems):
    start_pieces(halves, 0, raw_far, [piece], sems)[0].wait()


def add_kernel(halves, offset, raw, mine, received, *refs):
    total, *refs = refs[4:]
    pieces, sems = refs[:-1], refs[-1]
    copies = start_pieces(halves, offset, raw, pieces, sems)
    total[...] = mine[...] + received[...]
    for copy in copies:
        copy.wait()


def filter_modes(
    halves, half_turn, mine, other_a, other_b, far_mine, far_other,
    weight, correlation, edges, cutoff, starts, tables, modes, side, shifted, result,
):
    place = lax.axis_index("angle")
    odd = place % 2
    upper = place // halves
    half = KMAX // 2
    side[upper, odd] = mine[...]
    side[upper, 1 - odd] = other_a[...] + other_b[...]
    side[1 - upper, odd] = far_mine[...]
    side[1 - upper, 1 - odd] = far_other[...]

    def view(m):
        return lambda: (side[0, m // KMAX, m % KMAX], side[1, m // KMAX, m % KMAX])

    def emit(first, sheets):
        for i, sheet in enumerate(sheets):
            result[first + i] = sheet

    take_turns(
        transform_group(
            [view(m) for m in range(first, first + MODE_GROUP)],
            weight, correlation, edges, tables, tables["ramp_drop"], shifted, first, emit,
        )
        for first in range(0, MODES, MODE_GROUP)
    )
    cos, sin = rotations(place, starts, half_turn)
    for k in range(KMAX):
        spot = (k // half) * KMAX + k % half
        scale = jnp.where(k < cutoff, (1.0 if k == 0 else 2.0) / half_turn, 0.0)
        c = cos[k] * scale
        s = sin[k] * scale
        cos_sheet, sin_sheet = result[spot], result[spot + half]
        for row, sheet in (
            (k, cos_sheet * c + sin_sheet * s),
            (KMAX + k, sin_sheet * c - cos_sheet * s),
        ):
            high, low = split(sheet)
            for i in range(HALF_SIDE // 8):
                lanes = slice(i * SIDE, (i + 1) * SIDE)
                for part, value in enumerate((high, low, high)):
                    place_row = part * 8 * MODES + 8 * row
                    modes[place_row : place_row + 8, lanes] = value[8 * i : 8 * i + 8]


def low_sheets(basis, modes):
    low = dot(basis, modes)

    def block(i, j):
        return low[8 * i : 8 * i + 8, j * SIDE : (j + 1) * SIDE]

    return block


def clean_rows(
    halves, offset, groups, raw, partner, level, dark, weight, correlation, edges, tables, shifted, emit,
    beside=(),
):
    is_upper = lax.axis_index("angle") >= halves
    start = jnp.where(is_upper, raw.shape[0] // 2, 0) + offset

    def view(i):
        def load():
            here = level[...] - jnp.log(raw[start + i] - dark[...])
            there = level[...] - jnp.log(partner[i] - dark[...])
            return jnp.where(is_upper, there, here), jnp.where(is_upper, here, there)

        return load

    firsts = [sum(groups[:i]) for i in range(len(groups))]
    turns = [
        transform_group(
            [view(i) for i in range(first, first + size)],
            weight, correlation, edges, tables, tables["ramp"], shifted, first, emit,
        )
        for first, size in zip(firsts, groups)
    ]
    take_turns(turns + list(beside))


def prepare(settings, tables, shifted):
    shifted[:, :QUARTER, :] = jnp.zeros((shifted.shape[0], QUARTER, SIDE), F32)
    weight = blend_weight(settings[0], settings[1])
    return weight, edge_response(tables["edge"][...], settings[2])


def early_kernel(
    halves, offset, next_offset, groups, waits, raw, partner, level, dark, *refs,
):
    settings, refs = [ref[0] for ref in refs[:4]], refs[4:]
    refs = refs[waits:]
    names = TABLES + ("ramp",)
    tables = dict(zip(names, refs))
    out, *pieces, shifted, sems = refs[len(names) :]
    copies = start_pieces(halves, next_offset, raw, pieces, sems)
    weight, edges = prepare(settings, tables, shifted)

    def emit(first, sheets):
        for i, sheet in enumerate(sheets):
            out[first + i] = sheet

    clean_rows(
        halves, offset, groups, raw, partner, level, dark, weight, settings[0], edges, tables, shifted, emit
    )
    for copy in copies:
        copy.wait()


def middle_kernel(
    halves, half_turn, starts, early_count, mine, other_a, other_b, far_mine, far_other, basis,
    *refs,
):
    settings, refs = [ref[0] for ref in refs[:4]], refs[4:]
    names = TABLES + ("ramp_drop",)
    early, refs = refs[:early_count], refs[early_count:]
    tables = dict(zip(names, refs))
    fixed, modes, side, shifted, result = refs[len(names) :]
    weight, edges = prepare(settings, tables, shifted)
    filter_modes(
        halves, half_turn, mine, other_a, other_b, far_mine, far_other,
        weight, settings[0], edges, settings[3], starts, tables, modes, side, shifted, result,
    )
    low = low_sheets(basis[...], modes[...])
    row = 0
    for part in early:
        for i in range(part.shape[0]):
            for j in range(HALF_SIDE // 8):
                fixed[row, 8 * j : 8 * j + 8, :] = part[i, 8 * j : 8 * j + 8, :] - low(row, j)
            row += 1


class Joined:
    def __init__(self, refs):
        self.rows = [(ref, i) for ref in refs for i in range(ref.shape[0])]

    def __getitem__(self, row):
        ref, i = self.rows[row]
        return ref[i]


def late_kernel(
    halves, offset, groups, partner_count, writes, raw, level, dark, modes, basis, finished, *refs,
):
    settings, refs = [ref[0] for ref in refs[:4]], refs[4:]
    names = TABLES + ("ramp",)
    partner, refs = Joined(refs[:partner_count]), refs[partner_count:]
    tables = dict(zip(names, refs))
    refs = refs[len(names) :]
    out, done, shifted, sems = refs[1:] if writes else refs
    copies = []

    def send(source, first):
        target = out.at[pl.ds(first, source.shape[0])]
        copies.append(pltpu.make_async_copy(source, target, sems.at[len(copies)]))
        copies[-1].start()

    send(finished, offset - finished.shape[0])
    weight, edges = prepare(settings, tables, shifted)
    lows = []

    def low_turn():
        lows.append(low_sheets(basis[...], modes[...]))
        yield

    def emit(first, sheets):
        for i, sheet in enumerate(sheets):
            for j in range(HALF_SIDE // 8):
                done[first + i, 8 * j : 8 * j + 8, :] = (
                    sheet[8 * j : 8 * j + 8] - lows[0](first + i, j)
                )
        if writes:
            send(done.at[pl.ds(first, len(sheets))], offset + first)

    clean_rows(
        halves, offset, groups, raw, partner, level, dark, weight, settings[0], edges, tables, shifted, emit,
        [low_turn()],
    )
    for copy in copies:
        copy.wait()


VMEM_SPEC = pl.BlockSpec(memory_space=pltpu.VMEM)
SMEM_SPEC = pl.BlockSpec(memory_space=pltpu.SMEM)
ANY_SPEC = pl.BlockSpec(memory_space=pl.ANY)
MIB = 2**20
HEAD_COST = 16 * MIB


def call(kernel, name, operands, out_shape, out_specs, scratch, limit=32 * MIB, aliases=(), cost=0):
    specs = [spec for spec, _ in operands]
    return pl.pallas_call(
        kernel,
        out_shape=out_shape,
        in_specs=specs,
        out_specs=out_specs,
        scratch_shapes=scratch,
        input_output_aliases=dict(aliases),
        compiler_params=pltpu.CompilerParams(vmem_limit_bytes=limit),
        cost_estimate=pl.CostEstimate(flops=0, bytes_accessed=cost, transcendentals=0),
        name=name,
    )(*(value for _, value in operands))


def vmem(*values):
    return [(VMEM_SPEC, jnp.asarray(value)) for value in values]


def smem(*values):
    return [(SMEM_SPEC, jnp.asarray(value)) for value in values]


def table_operands(*extra):
    tables = transform_tables()
    return vmem(*(tables[name] for name in TABLES + extra))


def shifted_scratch(count):
    return pltpu.VMEM((count, 3 * QUARTER + 8, SIDE), F32)


def sheet_scratch(count):
    return pltpu.VMEM((count, HALF_SIDE, SIDE), F32)


def basis_pack(offset, count, half_turn):
    basis = np.kron(mode_basis(offset + count, half_turn)[offset:], np.eye(8))
    hi, lo = np_split(basis)
    return np.concatenate([hi, hi, lo], axis=1)


def far(*values):
    return [
        (ANY_SPEC, pltpu.with_memory_space_constraint(jnp.asarray(value), pltpu.HBM))
        for value in values
    ]


def piece_shapes(raw, counts):
    return [jax.ShapeDtypeStruct((count,) + raw.shape[1:], F32) for count in counts]


def head(raw, flat, dark, halves, half_turn):
    block = raw.shape[0] // 4
    hi, lo = np_split(np.kron(mode_basis(block, half_turn).T, np.eye(8)))
    basis = np.concatenate([hi, hi, lo], axis=1)
    shapes = [jax.ShapeDtypeStruct((KMAX, QUARTER, SIDE), F32)] * 2
    shapes += [jax.ShapeDtypeStruct((QUARTER, SIDE), F32)] * 2
    return call(
        functools.partial(head_kernel, halves, half_turn), "head",
        far(raw, flat, dark, basis), shapes, [VMEM_SPEC] * len(shapes),
        [
            pltpu.VMEM(raw.shape, F32),
            pltpu.VMEM(flat.shape, F32),
            pltpu.VMEM(basis.shape, BF16),
            pltpu.SemaphoreType.DMA((7,)),
        ],
        cost=HEAD_COST,
    )


def first_piece(raw, count, halves):
    return call(
        functools.partial(piece_kernel, halves), "first_piece", far(raw),
        piece_shapes(raw, [count])[0], VMEM_SPEC, [pltpu.SemaphoreType.DMA((1,))],
    )


def add_modes(raw, mine, received, settings, counts, offset, halves):
    shapes = [jax.ShapeDtypeStruct(mine.shape, F32)] + piece_shapes(raw, counts)
    return call(
        functools.partial(add_kernel, halves, offset), "add_modes",
        vmem(raw, mine, received) + smem(*settings),
        shapes, [VMEM_SPEC] * len(shapes), [pltpu.SemaphoreType.DMA((len(counts),))],
    )


def early_sheets(raw, partner, level, dark, after, settings, groups, offset, counts, next_offset, halves):
    operands = vmem(raw, partner, level, dark) + smem(*settings)
    operands += [(ANY_SPEC, value) for value in after] + table_operands("ramp")
    shapes = [jax.ShapeDtypeStruct((sum(groups), HALF_SIDE, SIDE), F32)] + piece_shapes(raw, counts)
    return call(
        functools.partial(early_kernel, halves, offset, next_offset, groups, len(after)), "early_sheets",
        operands, shapes, [VMEM_SPEC] * len(shapes),
        [shifted_scratch(sum(groups)), pltpu.SemaphoreType.DMA((max(len(counts), 1),))],
    )


def middle_sheets(early, parts, settings, halves, half_turn, half_block):
    count = sum(part.shape[0] for part in early)
    place = np.arange(2 * halves)
    starts = place % halves * 2 * half_block + place // halves * half_block
    operands = vmem(*parts, basis_pack(0, count, half_turn)) + smem(*settings)
    operands += vmem(*early) + table_operands("ramp_drop")
    return call(
        functools.partial(middle_kernel, halves, half_turn, starts, len(early)), "middle_sheets", operands,
        (
            jax.ShapeDtypeStruct((count, HALF_SIDE, SIDE), F32),
            jax.ShapeDtypeStruct((3 * 8 * MODES, HALF_SIDE // 8 * SIDE), BF16),
        ),
        (VMEM_SPEC, VMEM_SPEC),
        [
            pltpu.VMEM((2, 2, KMAX, QUARTER, SIDE), F32),
            shifted_scratch(MODES),
            sheet_scratch(MODES),
        ],
    )


def late_sheets(
    raw, partners, level, dark, modes, settings, groups, offset, halves, half_turn, finished, out=None,
):
    count = sum(groups)
    writes = out is not None
    operands = vmem(raw, level, dark, modes, basis_pack(offset, count, half_turn), finished)
    operands += smem(*settings) + vmem(*partners) + table_operands("ramp")
    aliases = {}
    if writes:
        aliases = {len(operands): 0}
        operands.append((ANY_SPEC, out))
    result = jax.ShapeDtypeStruct((raw.shape[0] // 2, HALF_SIDE, SIDE), F32)
    rows = jax.ShapeDtypeStruct((count, HALF_SIDE, SIDE), F32)
    scratch = [shifted_scratch(count), pltpu.SemaphoreType.DMA((1 + len(groups),))]
    return call(
        functools.partial(late_kernel, halves, offset, groups, len(partners), writes), "late_sheets",
        operands, [result] if writes else [result, rows],
        [ANY_SPEC] if writes else [ANY_SPEC, VMEM_SPEC],
        [sheet_scratch(count)] * writes + scratch, aliases=aliases,
    )


def local(intensity, flat_field, dark_field, correlation, blend_width, padding, cutoff):
    angle_count = lax.axis_size("angle")
    halves = angle_count // 2
    top_bit = angle_count.bit_length() - 2
    angles, local_rows, pixels = intensity.shape
    half_block = angles // 2
    half_turn = half_block * angle_count
    counts = [sum(groups) for groups in CHUNKS]
    starts = [sum(counts[:i]) for i in range(len(counts))]
    raw = intensity.reshape(angles, QUARTER, SIDE)
    partners = [swapped(first_piece(raw, counts[0], halves), "angle", top_bit)]
    mine, other, level, dark = head(
        raw, flat_field.reshape(QUARTER, SIDE), dark_field.reshape(QUARTER, SIDE), halves, half_turn
    )
    settings = (correlation, blend_width, padding, cutoff)
    for bit in range(1, top_bit):
        mine = mine + swapped(mine, "angle", bit)
        other = other + swapped(other, "angle", bit)
    received = swapped(other, "angle", 0)
    other_more = swapped(mine, "angle", 0)
    mine_sum, piece = add_modes(raw, mine, received, settings, counts[1:2], starts[1], halves)
    partners.append(swapped(piece, "angle", top_bit))
    far_mine = swapped(mine_sum, "angle", top_bit)
    first, *pieces = early_sheets(
        raw, partners[0], level, dark, (mine_sum, other_more), settings, CHUNKS[0], 0,
        counts[2:4], starts[2], halves,
    )
    partners += [swapped(piece, "angle", top_bit) for piece in pieces]
    far_other = swapped(far_mine, "angle", 0)
    second, *pieces = early_sheets(
        raw, partners[1], level, dark, (far_mine, first), settings, CHUNKS[1], starts[1],
        counts[4:], starts[4] if len(starts) > 4 else 0, halves,
    )
    partners += [swapped(piece, "angle", top_bit) for piece in pieces]
    early = [first, second]
    parts = (mine_sum, other, other_more, far_mine, far_other)
    fixed, modes = middle_sheets(early, parts, settings, halves, half_turn, half_block)
    out, late = late_sheets(
        raw, partners[2:3], level, dark, modes, settings, CHUNKS[2], starts[2],
        halves, half_turn, fixed,
    )
    (out,) = late_sheets(
        raw, partners[3:], level, dark, modes, settings, CHUNKS[3] + CHUNKS[4], starts[3],
        halves, half_turn, late, out,
    )
    return out.reshape(half_block, local_rows, 2 * pixels)


def solution(mesh):
    placed = (P("angle", "row", None), P("row", None), P("row", None), P(), P(), P(), P())
    return jax.shard_map(
        local, mesh=mesh, in_specs=placed, out_specs=P("angle", "row", None), check_vma=False
    )
```
